32 devices in a mesh: groups: 2 (over x), inst: 16 (over z, y, core).
Axes of the slice: x: 2, y: 2, z: 4, core: 2. Of those that a mesh axis runs over, the one named last changes fastest.
Arguments:
- hidden: bfloat16 [1024, 8192], P('groups', 'inst'), parts along dimension 0, may hold values from -64 to 64
- gain: float32 [8192], replicated, may hold values from 0.1 to 1.9
- w_query: bfloat16 [8192, 2048], P(None, 'inst'), may hold values from -0.0625 to 0.0625
- w_key: bfloat16 [8192, 256], P(None, 'inst'), may hold values from -0.0625 to 0.0625
- w_value: bfloat16 [8192, 256], P(None, 'inst'), may hold values from -0.0625 to 0.0625
- cache_pool: bfloat16 [1024, 64, 2, 256], P(('groups', 'inst')), parts along dimension 0, may hold values from -70 to 70
- prefix_len: int32 [4], P('groups'), parts along dimension 0, may hold values from 1024 to 4096, as said below
- hit_page: int32 [4, 64], P('groups'), parts along dimension 0, may hold values from -1 to 511, as said below
- decode_owner: int32 [32], P('groups'), parts along dimension 0, may hold values from 0 to 15, as said below
Outputs:
- attn_out: bfloat16 [1024, 2048], P('groups', 'inst'), parts along dimension 0
- decode_pages: bfloat16 [64, 64, 2, 128], P(('groups', 'inst')), parts along dimension 0
The draws below stay inside these ranges and needn't reach their ends.
There are 2 independent parts, one for each index of `groups`. The reference program is written for one: setup_inputs(seed, part) draws one part's arguments, and reference() takes and returns one part's arrays. A program takes and returns all parts, laid end to end along the dimension named above; an argument that names none is the same for every part. Nothing has to cross between parts.
Inputs may be any that keep to these rules, and one draw needn't show every extreme that they name: `prefix_len`: the largest length is exactly 4096. `hit_page`: an entry is -1 exactly for page entries p >= ceil(prefix_len[r] / 64); other entries are distinct pool pages, held by holder id // 32. No holder holds more than 16 entries of the list, and some holder holds exactly 16. `decode_owner`: no device owns more than 2 rows, and some device owns exactly 2.
All inputs are finite; a program needn't handle non-finite values.
Results may differ from the reference program's by a relative error of at most 0.007.
The reference program's roundings to bfloat16 on the way (of `normed` and `probs`) count: a program that leaves them out, or rounds other values in their place, can miss the bound.
Values may be sent and summed in bfloat16 or wider, within the bound.
No kernel may reach another device: no remote copies, remote signals or barrier semaphores. Data moves between devices by JAX's collectives and lax.ppermute only.
A program may use at most 128 MiB of HBM per device.

```python
import math
import jax
import jax.numpy as jnp
from jax import lax

D = 8192
HD = 128
HEADS = 16
KVH = 2
KVD = 256
REQS = 2
NEW_TOK = 256
PAGE = 64
PREFIX = 4096
MAXP = 64
TOKENS = 512
HITS = 16
POOL_DEV = 32
OWN = 2
ROWS_NEW = 16
N_INST = 16


def prefix_layout(key):
    subkeys = jax.random.split(key, 5)
    entries = REQS * MAXP
    lengths = jax.random.randint(subkeys[0], (REQS,), PREFIX // 4, PREFIX + 1)
    longest = jax.random.randint(subkeys[1], (), 0, REQS)
    lengths = jnp.where(jnp.arange(REQS) == longest, PREFIX, lengths).astype(jnp.int32)
    full_holder = jax.random.randint(subkeys[2], (), 0, N_INST)
    others = (full_holder + 1 + jnp.arange((N_INST - 1) * HITS) // HITS) % N_INST
    others = jax.random.permutation(subkeys[3], others)
    position = jnp.arange(entries)
    forced = (position // MAXP == longest) & (position % MAXP < HITS)
    before = jnp.clip(position - longest * MAXP, 0, HITS)
    taken_at = jnp.clip(position - before, 0, (N_INST - 1) * HITS - 1)
    holder = jnp.where(forced, full_holder, others[taken_at])
    earlier = (holder[None, :] == holder[:, None]) & (position[None, :] < position[:, None])
    ranking = jnp.sum(earlier.astype(jnp.int32), axis=1)
    offset = jax.random.randint(subkeys[4], (N_INST,), 0, POOL_DEV)
    pool_slot = (ranking + offset[holder]) % POOL_DEV
    used_pages = (lengths + PAGE - 1) // PAGE
    is_valid = position % MAXP < used_pages[position // MAXP]
    page_ids = jnp.where(is_valid, holder * POOL_DEV + pool_slot, -1)
    return (lengths, page_ids.reshape(REQS, MAXP).astype(jnp.int32))


def draw_prefix_len(key, part):
    lengths, page_ids = prefix_layout(key)
    return lengths


def draw_hit_page(key, part):
    lengths, page_ids = prefix_layout(key)
    return page_ids


def draw_decode_owner(key, part):
    key = jax.random.fold_in(key, 17)
    subkeys = jax.random.split(key, 3)
    shuffled = jax.random.permutation(subkeys[0], N_INST)
    pair_count = ROWS_NEW // 2
    shared = jax.random.randint(subkeys[1], (pair_count,), 0, 2)
    forced = jax.random.randint(subkeys[2], (), 0, pair_count)
    shared = jnp.where(jnp.arange(pair_count) == forced, 1, shared)
    even_rows = shuffled[0:ROWS_NEW:2]
    odd_rows = shuffled[1:ROWS_NEW:2]
    odd_rows = jnp.where(shared == 1, even_rows, odd_rows)
    return jnp.stack([even_rows, odd_rows], axis=1).reshape(ROWS_NEW).astype(jnp.int32)


def draw_hidden(key, part):
    key = jax.random.fold_in(key, 11)
    column = jnp.arange(D, dtype=jnp.float32) / D
    values = jax.random.truncated_normal(key, -5.0, 5.0, (TOKENS, D), jnp.float32)
    return (values * jnp.exp(math.log(3.0) * column)).astype(jnp.bfloat16)


def draw_cache_pool(key, part):
    key = jax.random.fold_in(key, 13)
    shape = (N_INST * POOL_DEV, PAGE, 2, KVD)
    return jax.random.truncated_normal(key, -5.0, 5.0, shape, jnp.float32).astype(jnp.bfloat16)


def levels(own_key, dims, cuts, least, high):
    def one(dim, shards_of):
        heights = jax.random.uniform(jax.random.fold_in(jax.random.fold_in(own_key, 6), dim), (shards_of,), jnp.float32, least / len(cuts), high / len(cuts))
        return jnp.repeat(jnp.exp(heights), dims[dim] // shards_of).reshape((-1,) + (1,) * (len(dims) - dim - 1))

    loudness = one(*cuts[0])
    for cut in cuts[1:]:
        loudness = loudness * one(*cut)
    return loudness


def normal_values(stream_key, shape, width, reach, cuts=(), kind=jnp.bfloat16):
    factor_of = levels(stream_key, shape, cuts, -0.22, 0.18) if cuts else 1.0
    values = jax.random.normal(stream_key, shape, jnp.float32) * width * factor_of
    return jnp.minimum(jnp.maximum(values, -reach), reach).astype(kind)


def setup_inputs(seed: int = 0, part: int = 0) -> dict:
    streams_of = jax.random.split(jax.random.key(seed), 10)
    part_keys = jax.random.split(jax.random.fold_in(streams_of[9], part), 10)
    return {
        "hidden": draw_hidden(jax.random.fold_in(jax.random.fold_in(streams_of[9], part), 71), part),
        "gain": jnp.clip(1.0 + 0.18 * jax.random.normal(streams_of[1], (D,), jnp.float32), 0.1, 1.9),
        "w_query": normal_values(streams_of[2], (D, HEADS * HD), D ** -0.5, 0.0625, ((1, 16),)),
        "w_key": normal_values(streams_of[3], (D, KVD), D ** -0.5, 0.0625, ((1, 16),)),
        "w_value": normal_values(streams_of[4], (D, KVD), D ** -0.5, 0.0625, ((1, 16),)),
        "cache_pool": draw_cache_pool(jax.random.fold_in(jax.random.fold_in(streams_of[9], part), 71), part),
        "prefix_len": draw_prefix_len(jax.random.fold_in(jax.random.fold_in(streams_of[9], part), 71), part),
        "hit_page": draw_hit_page(jax.random.fold_in(jax.random.fold_in(streams_of[9], part), 71), part),
        "decode_owner": draw_decode_owner(jax.random.fold_in(jax.random.fold_in(streams_of[9], part), 71), part),
    }


EPS = 1e-05
ROPE_BASE = 500000.0

def rotary_tables(positions):
    half_dim = HD // 2
    freqs = ROPE_BASE ** (-(jnp.arange(half_dim, dtype=jnp.float32) * 2.0 / HD))
    angles = positions[:, None] * freqs[None, :]
    return (jnp.cos(angles), jnp.sin(angles))

def rotate_rows(values, cos_table, sin_table):
    half_dim = values.shape[-1] // 2
    first_half = values[..., :half_dim]
    second_half = values[..., half_dim:]
    return jnp.concatenate([first_half * cos_table - second_half * sin_table, second_half * cos_table + first_half * sin_table], axis=-1)

def group_attention(q_group, key_rows, value_rows, allowed):
    scores = jnp.einsum('hqd,kd->hqk', q_group.astype(jnp.float32), key_rows.astype(jnp.float32)) * HD ** (-0.5)
    row_max = lax.optimization_barrier(jnp.max(jnp.where(allowed, scores, -jnp.inf), axis=-1, keepdims=True))
    exps = jnp.where(allowed, jnp.exp(scores - row_max), 0.0)
    row_sum = lax.optimization_barrier(jnp.sum(exps, axis=-1, keepdims=True))
    probs = exps.astype(jnp.bfloat16)
    mixture = jnp.einsum('hqk,kd->hqd', probs.astype(jnp.float32), value_rows.astype(jnp.float32))
    return (mixture / row_sum).astype(jnp.bfloat16)

def reference(hidden, gain, w_query, w_key, w_value, cache_pool, prefix_len, hit_page, decode_owner):
    wide_vals = hidden.astype(jnp.float32)
    inverse_rms = lax.rsqrt(lax.optimization_barrier(jnp.mean(wide_vals * wide_vals, axis=-1, keepdims=True)) + EPS)
    normed = (wide_vals * inverse_rms * gain).astype(jnp.bfloat16)
    query = jnp.dot(normed, w_query, preferred_element_type=jnp.float32)
    key_new = jnp.dot(normed, w_key, preferred_element_type=jnp.float32).astype(jnp.bfloat16)
    value_new = jnp.dot(normed, w_value, preferred_element_type=jnp.float32).astype(jnp.bfloat16)
    position = jnp.arange(TOKENS, dtype=jnp.int32)
    positions = (prefix_len[position // NEW_TOK] + position % NEW_TOK).astype(jnp.float32)
    cos_table, sin_table = rotary_tables(positions)
    q_rot = rotate_rows(query.reshape(TOKENS, HEADS, HD).transpose(1, 0, 2), cos_table, sin_table).astype(jnp.bfloat16)
    k_rot = rotate_rows(key_new.astype(jnp.float32).reshape(TOKENS, KVH, HD).transpose(1, 0, 2), cos_table, sin_table).astype(jnp.bfloat16)
    v_heads = value_new.reshape(TOKENS, KVH, HD).transpose(1, 0, 2)
    pool_rows = cache_pool[jnp.maximum(hit_page, 0)].reshape(REQS, PREFIX, 2, KVH, HD)
    prefix_keys = pool_rows[:, :, 0]
    prefix_values = pool_rows[:, :, 1]
    group_size = HEADS // KVH
    outputs = []
    for request in range(REQS):
        prefix_ok = jnp.broadcast_to(jnp.arange(PREFIX, dtype=jnp.int32)[None, :] < prefix_len[request], (NEW_TOK, PREFIX))
        causal_ok = jnp.arange(NEW_TOK, dtype=jnp.int32)[None, :] <= jnp.arange(NEW_TOK, dtype=jnp.int32)[:, None]
        allowed = jnp.concatenate([prefix_ok, causal_ok], axis=1)
        start = request * NEW_TOK

        def per_group(group):
            first_head = (group * group_size).astype(jnp.int32)
            q_group = lax.dynamic_slice(q_rot, (first_head, jnp.asarray(start, dtype=jnp.int32), jnp.asarray(0, dtype=jnp.int32)), (group_size, NEW_TOK, HD))
            key_rows = jnp.concatenate([lax.dynamic_index_in_dim(prefix_keys[request], group, 1, keepdims=False), lax.dynamic_index_in_dim(k_rot, group, 0, keepdims=False)[start:start + NEW_TOK]], axis=0)
            value_rows = jnp.concatenate([lax.dynamic_index_in_dim(prefix_values[request], group, 1, keepdims=False), lax.dynamic_index_in_dim(v_heads, group, 0, keepdims=False)[start:start + NEW_TOK]], axis=0)
            return group_attention(q_group, key_rows, value_rows, allowed)
        per_heads = lax.map(per_group, jnp.arange(KVH, dtype=jnp.int32))
        outputs.append(per_heads.reshape(HEADS, NEW_TOK, HD).transpose(1, 0, 2).reshape(NEW_TOK, HEADS * HD))
    attn_out = jnp.concatenate(outputs, axis=0)
    pages_new = NEW_TOK // PAGE
    k_pages = k_rot.reshape(KVH, REQS, pages_new, PAGE, HD).transpose(1, 2, 0, 3, 4).reshape(ROWS_NEW, PAGE, HD)
    v_pages = v_heads.reshape(KVH, REQS, pages_new, PAGE, HD).transpose(1, 2, 0, 3, 4).reshape(ROWS_NEW, PAGE, HD)
    page_rows = jnp.stack([k_pages, v_pages], axis=2)
    row_ids = jnp.arange(ROWS_NEW, dtype=jnp.int32)
    earlier = (decode_owner[None, :] == decode_owner[:, None]) & (row_ids[None, :] < row_ids[:, None])
    slot_num = lax.optimization_barrier(jnp.sum(earlier.astype(jnp.int32), axis=1))
    target = (decode_owner * OWN + slot_num).astype(jnp.int32)
    decode_pages = jnp.zeros((N_INST * OWN, PAGE, 2, HD), jnp.bfloat16).at[target].set(page_rows)
    return (attn_out, decode_pages)
```

```python
import functools

import jax
import jax.numpy as jnp
from jax import lax
from jax.experimental import pallas as pl
from jax.experimental.pallas import tpu as pltpu
from jax.sharding import PartitionSpec as P

OWN = 2


EPS = 1e-05
ROPE_BASE = 500000.0


def rotary_tables(positions, head_dim):
    half_dim = head_dim // 2
    freqs = ROPE_BASE ** (-(jnp.arange(half_dim, dtype=jnp.float32) * 2.0 / head_dim))
    angles = positions[:, None] * freqs[None, :]
    return (jnp.cos(angles), jnp.sin(angles))


def rotate_rows(values, cos_table, sin_table):
    half_dim = values.shape[-1] // 2
    first_half = values[..., :half_dim]
    second_half = values[..., half_dim:]
    return jnp.concatenate(
        [
            first_half * cos_table - second_half * sin_table,
            second_half * cos_table + first_half * sin_table,
        ],
        axis=-1,
    )


def rotate_cols(values, cos_table, sin_table):
    half_dim = values.shape[-2] // 2
    first_half = values[..., :half_dim, :]
    second_half = values[..., half_dim:, :]
    return jnp.concatenate(
        [
            first_half * cos_table - second_half * sin_table,
            second_half * cos_table + first_half * sin_table,
        ],
        axis=-2,
    )


def contract_last(left, right):
    return lax.dot_general(
        left, right, (((1,), (1,)), ((), ())), preferred_element_type=jnp.float32
    )


def contract_first(weights, rows):
    return lax.dot_general(
        weights, rows, (((0,), (1,)), ((), ())), preferred_element_type=jnp.float32
    )


def on_device(
    hidden, gain, w_query, w_key, w_value, cache_pool, prefix_len, hit_page, decode_owner
):
    my_index = lax.axis_index("inst")
    devices = lax.axis_size("inst")
    tok_count = hidden.shape[0]
    head_dim = w_query.shape[1]
    requests = prefix_len.shape[0]
    new_len = tok_count // requests
    gathered = lax.all_gather(hidden, "inst", axis=1, tiled=True)
    wide_vals = gathered.astype(jnp.float32)
    inverse_rms = lax.rsqrt(jnp.mean(wide_vals * wide_vals, axis=-1, keepdims=True) + EPS)
    normed = (wide_vals * inverse_rms * gain).astype(jnp.bfloat16)
    query = jnp.dot(normed, w_query, preferred_element_type=jnp.float32)
    key_cols = contract_first(w_key, normed)
    value_cols = contract_first(w_value, normed)
    new_kv = jnp.stack([key_cols.astype(jnp.bfloat16), value_cols.astype(jnp.bfloat16)])
    all_kv = lax.all_gather(new_kv, "inst", axis=1, tiled=True)
    kv_dim = all_kv.shape[1]
    kv_heads = kv_dim // head_dim
    group_size = devices // kv_heads
    my_group = my_index // group_size
    positions = (
        jnp.repeat(prefix_len, new_len) + jnp.tile(jnp.arange(new_len, dtype=jnp.int32), requests)
    ).astype(jnp.float32)
    cos_table, sin_table = rotary_tables(positions, head_dim)
    q_rot = rotate_rows(query, cos_table, sin_table).astype(jnp.bfloat16)
    k_rot = rotate_cols(
        all_kv[0].astype(jnp.float32).reshape(kv_heads, head_dim, tok_count),
        cos_table.T,
        sin_table.T,
    ).astype(jnp.bfloat16)
    v_heads = all_kv[1].reshape(kv_heads, head_dim, tok_count)
    my_keys = lax.dynamic_index_in_dim(k_rot, my_group, 0, keepdims=False)
    my_values = lax.dynamic_index_in_dim(v_heads, my_group, 0, keepdims=False)
    pool_dev = cache_pool.shape[0]
    page_len = cache_pool.shape[1]
    hit_slots = pool_dev // 2
    flat_hits = hit_page.reshape(-1)
    entries = flat_hits.shape[0]
    is_valid = flat_hits >= 0
    holder = jnp.where(is_valid, flat_hits // pool_dev, -1)
    pool_slot = jnp.where(is_valid, flat_hits % pool_dev, 0)
    entry_ids = jnp.arange(entries, dtype=jnp.int32)
    earlier = (
        (holder[None, :] == holder[:, None])
        & (entry_ids[None, :] < entry_ids[:, None])
        & is_valid[None, :]
    )
    ranking = jnp.sum(earlier.astype(jnp.int32), axis=1)
    mine = is_valid & (holder == my_index)
    chosen = mine[None, :] & (ranking[None, :] == jnp.arange(hit_slots, dtype=jnp.int32)[:, None])
    pool_index = jnp.sum(jnp.where(chosen, pool_slot[None, :], 0), axis=1)
    present = jnp.any(chosen, axis=1)
    picked = cache_pool[pool_index]
    picked = jnp.where(present[:, None, None, None], picked, jnp.zeros_like(picked))
    inv_scale = head_dim ** (-0.5)
    per_head = picked.reshape(hit_slots, page_len, 2, kv_heads, head_dim).transpose(3, 0, 1, 2, 4)
    outgoing = jnp.repeat(per_head, group_size, axis=0)
    incoming = lax.all_to_all(outgoing, "inst", split_axis=0, concat_axis=0, tiled=True)
    stacked = incoming.reshape(devices * hit_slots, page_len, 2, head_dim)
    where_from = jnp.where(is_valid, holder * hit_slots + ranking, 0)
    prefix_rows = stacked[where_from]
    prefix_keys = prefix_rows[:, :, 0].reshape(requests, -1, head_dim)
    prefix_values = prefix_rows[:, :, 1].reshape(requests, -1, head_dim)
    prefix_span = prefix_keys.shape[1]
    causal_ok = (
        jnp.arange(new_len, dtype=jnp.int32)[None, :]
        <= jnp.arange(new_len, dtype=jnp.int32)[:, None]
    )
    pieces = []
    for request in range(requests):
        lower = request * new_len
        q_part = q_rot[lower : lower + new_len]
        pre_scores = contract_last(q_part, prefix_keys[request]) * inv_scale
        new_scores = (
            jnp.dot(q_part, my_keys[:, lower : lower + new_len], preferred_element_type=jnp.float32)
            * inv_scale
        )
        prefix_ok = jnp.arange(prefix_span, dtype=jnp.int32)[None, :] < prefix_len[request]
        row_max = jnp.maximum(
            jnp.max(jnp.where(prefix_ok, pre_scores, -jnp.inf), axis=1),
            jnp.max(jnp.where(causal_ok, new_scores, -jnp.inf), axis=1),
        )[:, None]
        pre_exps = jnp.where(prefix_ok, jnp.exp(pre_scores - row_max), 0.0)
        new_exps = jnp.where(causal_ok, jnp.exp(new_scores - row_max), 0.0)
        row_sum = jnp.sum(pre_exps, axis=1, keepdims=True) + jnp.sum(
            new_exps, axis=1, keepdims=True
        )
        mixture = jnp.dot(
            pre_exps.astype(jnp.bfloat16),
            prefix_values[request],
            preferred_element_type=jnp.float32,
        )
        mixture = mixture + contract_last(
            new_exps.astype(jnp.bfloat16), my_values[:, lower : lower + new_len]
        )
        pieces.append((mixture / row_sum).astype(jnp.bfloat16))
    attn_out = jnp.concatenate(pieces, axis=0)
    pages_new = new_len // page_len
    rows_new = decode_owner.shape[0]
    k_pages = (
        k_rot.reshape(kv_heads, head_dim, requests, pages_new, page_len)
        .transpose(2, 3, 0, 4, 1)
        .reshape(rows_new, page_len, head_dim)
    )
    v_pages = (
        v_heads.reshape(kv_heads, head_dim, requests, pages_new, page_len)
        .transpose(2, 3, 0, 4, 1)
        .reshape(rows_new, page_len, head_dim)
    )
    row_ids = jnp.arange(rows_new, dtype=jnp.int32)
    before_rows = (decode_owner[None, :] == decode_owner[:, None]) & (
        row_ids[None, :] < row_ids[:, None]
    )
    slot_num = jnp.sum(before_rows.astype(jnp.int32), axis=1)
    owned = (decode_owner[None, :] == my_index) & (
        slot_num[None, :] == jnp.arange(OWN, dtype=jnp.int32)[:, None]
    )
    pick_row = jnp.sum(jnp.where(owned, row_ids[None, :], 0), axis=1)
    has_row = jnp.any(owned, axis=1)
    page_pair = jnp.stack([k_pages[pick_row], v_pages[pick_row]], axis=2)
    decode_pages = jnp.where(has_row[:, None, None, None], page_pair, jnp.zeros_like(page_pair))
    return (attn_out, decode_pages)


VMEM_LIMIT = 48 * 1024 * 1024


def in_vmem(count):
    return [pl.BlockSpec(memory_space=pltpu.VMEM)] * count


def in_smem(count):
    return [pl.BlockSpec(memory_space=pltpu.SMEM)] * count


def params():
    return pltpu.CompilerParams(vmem_limit_bytes=VMEM_LIMIT)


def cost(flops, nbytes):
    return pl.CostEstimate(flops=flops, bytes_accessed=nbytes, transcendentals=0)


def nt_dot(left, right):
    return lax.dot_general(
        left, right, (((1,), (1,)), ((), ())), preferred_element_type=jnp.float32
    )


def pick_pages_kernel(slots, place_ref, hits_ref, pool_ref, mine_ref, other_ref):
    me, head = place_ref[0], place_ref[1]
    pool_dev, page_len = pool_ref.shape[0], pool_ref.shape[1]
    rows = 2 * page_len
    out_row = lax.broadcasted_iota(jnp.int32, (rows, rows), 0)
    in_row = lax.broadcasted_iota(jnp.int32, (rows, rows), 1)
    wanted = jnp.where(out_row < page_len, 2 * out_row, 2 * (out_row - page_len) + 1)
    unweave = (in_row == wanted).astype(jnp.bfloat16)

    def entry(e, count):
        page = hits_ref[e]
        is_mine = (page >= 0) & (page // pool_dev == me)

        @pl.when(is_mine)
        def _():
            at = pl.ds(pl.multiple_of(count * rows, rows), rows)
            slab = pool_ref[page - me * pool_dev]
            first = slab[:, :, :128].reshape(rows, 128)
            second = slab[:, :, 128:].reshape(rows, 128)
            both = jnp.concatenate([first, second], axis=1)
            both = jnp.dot(unweave, both, preferred_element_type=jnp.float32)
            both = both.astype(jnp.bfloat16)
            mine_ref[at, :] = jnp.where(head == 0, both[:, :128], both[:, 128:])
            other_ref[at, :] = jnp.where(head == 0, both[:, 128:], both[:, :128])

        return count + is_mine.astype(jnp.int32)

    lax.fori_loop(0, hits_ref.shape[0], entry, jnp.int32(0))


def pick_pages(place, hits, pool, slots):
    rows = slots * 2 * pool.shape[1]
    block = jax.ShapeDtypeStruct((rows, 128), jnp.bfloat16)
    return pl.pallas_call(
        functools.partial(pick_pages_kernel, slots),
        out_shape=(block, block),
        in_specs=in_smem(2) + in_vmem(1),
        out_specs=tuple(in_vmem(2)),
        compiler_params=params(),
        cost_estimate=cost(0, 4 * pool.size),
        name="pick_pages",
    )(place, hits, pool)


def pack_weights_kernel(place_ref, wq_ref, wk_ref, wv_ref, *out_refs):
    plane, lane = place_ref[2], place_ref[3]
    feats = wk_ref.shape[0]
    block = wq_ref.shape[0] // 16
    for r, out_ref in enumerate(out_refs):
        for k in range(4):
            start = (lax.rem(plane + k, 4) * 4 + (lane ^ r)) * block
            start = pl.multiple_of(start, block)
            out_ref[k * block : (k + 1) * block, :] = wq_ref[pl.ds(start, block), :]
            for j in range(block // 128):
                at = 4 * block + (k * (block // 128) + j) * 2 * feats
                columns = pl.ds(pl.multiple_of(start + j * 128, 128), 128)
                out_ref[at : at + feats, :] = wk_ref[:, columns]
                out_ref[at + feats : at + 2 * feats, :] = wv_ref[:, columns]


def pack_weights(place, wq, wk_t, wv_t):
    rows = wq.shape[0] // 4 + 2 * wk_t.shape[0] * wk_t.shape[1] // 4 // 128
    block = jax.ShapeDtypeStruct((rows, 128), jnp.bfloat16)
    return pl.pallas_call(
        pack_weights_kernel,
        out_shape=(block,) * 4,
        in_specs=in_smem(1) + in_vmem(3),
        out_specs=tuple(in_vmem(4)),
        compiler_params=params(),
        cost_estimate=cost(0, 4 * wq.size),
        name="pack_weights",
    )(place, wq, wk_t, wv_t)


def project_kernel(place_ref, inv_ref, gain_ref, *refs):
    plane = place_ref[2]
    own_ref, downs, ups = refs[0], refs[1:4], refs[4:7]
    weights, (near_ref, far_ref) = refs[7:11], refs[11:13]
    toks, block = own_ref.shape
    chunks = block // 128
    inv = inv_ref[...]
    totals = [None] * 4
    kv_total = None
    for k in range(4):
        if k == 0:
            raw = own_ref[...]
        else:
            raw = jnp.where(plane + k <= 3, downs[k - 1][...], ups[3 - k][...])
        normed = (raw.astype(jnp.float32) * inv * gain_ref[k : k + 1, :]).astype(jnp.bfloat16)
        kv_rows = []
        for r in range(4):
            part = jnp.dot(
                normed,
                weights[r][k * block : (k + 1) * block, :],
                preferred_element_type=jnp.float32,
            )
            totals[r] = part if k == 0 else totals[r] + part
            pieces = []
            for j in range(chunks):
                at = 4 * block + (k * chunks + j) * 32
                pieces.append(weights[r][at : at + 32, :])
            kv_rows.append(jnp.concatenate(pieces, axis=1))
        kv_part = nt_dot(jnp.concatenate(kv_rows, axis=0), normed)
        kv_total = kv_part if k == 0 else kv_total + kv_part
    for out_ref, lanes in ((near_ref, (0, 2)), (far_ref, (1, 3))):
        for n, r in enumerate(lanes):
            base = n * (toks + 128)
            out_ref[base : base + toks, :] = totals[r]
            for t in range(toks // 128):
                out_ref[base + toks + t * 32 : base + toks + (t + 1) * 32, :] = kv_total[
                    r * 32 : (r + 1) * 32, t * 128 : (t + 1) * 128
                ]


def project(place, inv, gain, own, downs, ups, weights):
    toks = own.shape[0]
    out = jax.ShapeDtypeStruct((2 * (toks + 128), 128), jnp.float32)
    return pl.pallas_call(
        project_kernel,
        out_shape=(out, out),
        in_specs=in_smem(1) + in_vmem(2 + 7 + 4),
        out_specs=tuple(in_vmem(2)),
        compiler_params=params(),
        cost_estimate=cost(2 * toks * 2048 * 640, 6 << 20),
        name="project",
    )(place, inv, gain, own, *downs, *ups, *weights)


def finish_kernel(left_ref, middle_ref, right_ref, cos_ref, sin_ref, out_ref):
    toks = cos_ref.shape[0]
    total = left_ref[: toks + 128, :] + middle_ref[: toks + 128, :] + right_ref[...]
    query = total[:toks]
    swapped = jnp.concatenate([query[:, 64:], query[:, :64]], axis=1)
    out_ref[:toks, :] = (query * cos_ref[...] + swapped * sin_ref[...]).astype(jnp.bfloat16)
    out_ref[toks:, :] = total[toks:].astype(jnp.bfloat16)


def finish(near, got, far_sum, cos_wide, sin_wide):
    toks = cos_wide.shape[0]
    return pl.pallas_call(
        finish_kernel,
        out_shape=jax.ShapeDtypeStruct((toks + 128, 128), jnp.bfloat16),
        in_specs=in_vmem(5),
        out_specs=in_vmem(1)[0],
        compiler_params=params(),
        cost_estimate=cost(0, 2 << 20),
        name="finish_projection",
    )(near, got, far_sum, cos_wide, sin_wide)


def sort_pages_kernel(place_ref, hits_ref, lens_ref, *refs):
    blocks, (keys_ref, values_ref, count_ref) = refs[:8], refs[8:11]
    held, seen, sems = refs[11:]
    me = place_ref[0]
    pool_dev = place_ref[4]
    copies = [
        pltpu.make_async_copy(block, held.at[n], sems.at[n]) for n, block in enumerate(blocks)
    ]
    for copy in copies:
        copy.start()
    requests, keys_max = keys_ref.shape[0], keys_ref.shape[1]
    entries = hits_ref.shape[0]
    per_request = entries // requests
    page_len = keys_max // per_request
    values_ref[...] = jnp.zeros_like(values_ref)
    keys_ref[...] = jnp.zeros_like(keys_ref)
    for h in range(16):
        seen[h] = 0
    for copy in copies:
        copy.wait()
    for request in range(requests):

        def entry(p, carry, request=request):
            pages, tokens = carry
            page = hits_ref[request * per_request + p]
            valid = page >= 0
            holder = jnp.maximum(page, 0) // pool_dev
            rel = holder ^ me
            taken = valid & ((rel & 4) == 0)
            slot = seen[holder]
            seen[holder] = slot + valid.astype(jnp.int32)

            @pl.when(taken)
            def _():
                which = ((rel >> 3) & 1) * 4 + (rel & 3)
                source = pl.multiple_of(slot * 2 * page_len, 2 * page_len)
                target = pl.multiple_of(pages * page_len, page_len)
                keys_ref[request, pl.ds(target, page_len), :] = held[
                    which, pl.ds(source, page_len), :
                ]
                values_ref[request, pl.ds(target, page_len), :] = held[
                    which, pl.ds(source + page_len, page_len), :
                ]

            here = taken.astype(jnp.int32)
            filled = jnp.minimum(page_len, lens_ref[request] - p * page_len)
            return pages + here, tokens + here * filled

        _, tokens = lax.fori_loop(0, per_request, entry, (jnp.int32(0), jnp.int32(0)))
        count_ref[request] = tokens


def sort_pages(place, hits, lens, blocks, page_len):
    requests = lens.shape[0]
    span = hits.shape[0] // requests * page_len
    side = jax.ShapeDtypeStruct((requests, span, 128), jnp.bfloat16)
    return pl.pallas_call(
        sort_pages_kernel,
        out_shape=(side, side, jax.ShapeDtypeStruct((requests,), jnp.int32)),
        in_specs=in_smem(3) + [pl.BlockSpec(memory_space=pl.ANY)] * 8,
        out_specs=tuple(in_vmem(2) + in_smem(1)),
        scratch_shapes=[
            pltpu.VMEM((8,) + blocks[0].shape, jnp.bfloat16),
            pltpu.SMEM((16,), jnp.int32),
            pltpu.SemaphoreType.DMA((8,)),
        ],
        compiler_params=params(),
        cost_estimate=cost(0, 8 << 20),
        name="sort_pages",
    )(place, hits, lens, *blocks)


def column_to_row(column):
    return jnp.transpose(jnp.broadcast_to(column, (128, 128)))[0:1]


def row_to_column(row):
    return jnp.transpose(jnp.broadcast_to(row, (128, 128)))[:, 0:1]


def attend_kernel(chunk, count_ref, query_ref, keys_ref, values_ref, out_ref, acc, top, total):
    requests = keys_ref.shape[0]
    toks = out_ref.shape[0] - 8
    new_len = toks // requests
    for request in range(requests):
        query = query_ref[request * new_len : (request + 1) * new_len, :]
        keys_here = count_ref[request]
        acc[...] = jnp.zeros_like(acc)
        top[...] = jnp.full_like(top, -jnp.inf)
        total[...] = jnp.zeros_like(total)

        def step(n, carry, request=request, query=query, keys_here=keys_here):
            at = pl.ds(pl.multiple_of(n * chunk, chunk), chunk)
            scores = nt_dot(query, keys_ref[request, at, :]) * 128**-0.5
            column = lax.broadcasted_iota(jnp.int32, scores.shape, 1)
            scores = jnp.where(column < keys_here - n * chunk, scores, -jnp.inf)
            old = top[:, 0:1]
            new = jnp.maximum(old, jnp.max(scores, axis=1, keepdims=True))
            exps = jnp.exp(scores - new)
            fade = jnp.exp(old - new)
            total[...] = total[...] * fade + jnp.sum(exps, axis=1, keepdims=True)
            acc[...] = acc[...] * fade + jnp.dot(
                exps.astype(jnp.bfloat16),
                values_ref[request, at, :],
                preferred_element_type=jnp.float32,
            )
            top[...] = jnp.broadcast_to(new, top.shape)
            return carry

        lax.fori_loop(0, (keys_here + chunk - 1) // chunk, step, 0)
        out_ref[request * new_len : (request + 1) * new_len, :] = acc[...]
        for b in range(new_len // 128):
            row = request * (new_len // 128) + b
            part = slice(b * 128, (b + 1) * 128)
            out_ref[toks + row : toks + row + 1, :] = column_to_row(top[part, 0:1])
            out_ref[toks + 4 + row : toks + 5 + row, :] = column_to_row(total[part, 0:1])


def attend(count, query_kv, keys, values, toks):
    new_len = toks // keys.shape[0]
    return pl.pallas_call(
        functools.partial(attend_kernel, 512),
        out_shape=jax.ShapeDtypeStruct((toks + 8, 128), jnp.float32),
        in_specs=in_smem(1) + in_vmem(3),
        out_specs=in_vmem(1)[0],
        scratch_shapes=[pltpu.VMEM((new_len, 128), jnp.float32)] * 3,
        compiler_params=params(),
        cost_estimate=cost(4 * new_len * 4096 * 128, 16 << 20),
        name="attend_prefix",
    )(count, query_kv, keys, values)


def new_tokens_kernel(
    place_ref, near_ref, side_ref, core_ref, cos_ref, sin_ref, key_ref, value_ref, page_ref, held, kt, vt
):
    me, head = place_ref[0], place_ref[1]
    toks = key_ref.shape[1]
    for n in range(4):
        held[n] = near_ref[n]
        held[4 + n] = side_ref[n]
    for n in range(8):
        held[8 + n] = core_ref[n]
    for device in range(16):
        rel = device ^ me
        block = held[(rel & 1) * 8 + ((rel >> 1) & 1) * 4 + (rel >> 2)]
        rows = slice((device % 8) * 16, (device % 8) * 16 + 16)
        for t in range(toks // 128):
            columns = slice(t * 128, (t + 1) * 128)
            kt[device // 8, rows, columns] = block[t * 32 : t * 32 + 16]
            vt[device // 8, rows, columns] = block[t * 32 + 16 : t * 32 + 32]
    cos, sin = cos_ref[...], sin_ref[...]
    for g in range(2):
        first = kt[g, :64, :].astype(jnp.float32)
        second = kt[g, 64:, :].astype(jnp.float32)
        kt[g, :64, :] = (first * cos - second * sin).astype(jnp.bfloat16)
        kt[g, 64:, :] = (second * cos + first * sin).astype(jnp.bfloat16)
    key_ref[...] = kt[head]
    value_ref[...] = vt[head]
    page_len = page_ref.shape[1]
    out_row = lax.broadcasted_iota(jnp.int32, (2 * page_len, 128), 0)
    token = lax.broadcasted_iota(jnp.int32, (2 * page_len, 128), 1)
    for slot in range(page_ref.shape[0]):
        row, has = place_ref[5 + 2 * slot], place_ref[6 + 2 * slot]
        start = (row // 8) * (toks // 2) + ((row // 2) % 4) * page_len
        columns = pl.ds(pl.multiple_of(start // 128 * 128, 128), 128)
        inside = token - start % 128
        inside = jnp.where(has > 0, inside, -1)
        take_k = ((out_row % 2 == 0) & (inside == out_row // 2)).astype(jnp.bfloat16)
        take_v = ((out_row % 2 == 1) & (inside == out_row // 2)).astype(jnp.bfloat16)
        woven = nt_dot(take_k, kt[row % 2, :, columns]) + nt_dot(take_v, vt[row % 2, :, columns])
        page_ref[slot] = woven.astype(jnp.bfloat16).reshape(page_len, 2, 128)


def new_tokens(place, near, side, core, cos_t, sin_t, page_len):
    toks = cos_t.shape[1]
    half = jax.ShapeDtypeStruct((128, toks), jnp.bfloat16)
    return pl.pallas_call(
        new_tokens_kernel,
        out_shape=(half, half, jax.ShapeDtypeStruct((OWN, page_len, 2, 128), jnp.bfloat16)),
        in_specs=in_smem(1) + in_vmem(5),
        out_specs=tuple(in_vmem(3)),
        scratch_shapes=[
            pltpu.VMEM((16, 128, 128), jnp.bfloat16),
            pltpu.VMEM((2, 128, toks), jnp.bfloat16),
            pltpu.VMEM((2, 128, toks), jnp.bfloat16),
        ],
        compiler_params=params(),
        cost_estimate=cost(0, 2 << 20),
        name="new_tokens",
    )(place, near, side, core, cos_t, sin_t)


def combine_kernel(own_ref, far_ref, query_ref, key_ref, value_ref, out_ref):
    toks = out_ref.shape[0]
    new_len = toks // 2
    query_at = lax.broadcasted_iota(jnp.int32, (128, new_len), 0)
    key_at = lax.broadcasted_iota(jnp.int32, (128, new_len), 1)
    for b in range(toks // 128):
        rows = slice(b * 128, (b + 1) * 128)
        request = b * 128 // new_len
        columns = slice(request * new_len, (request + 1) * new_len)
        scores = jnp.dot(query_ref[rows, :], key_ref[:, columns], preferred_element_type=jnp.float32)
        allowed = key_at <= query_at + (b * 128 - request * new_len)
        scores = jnp.where(allowed, scores * 128**-0.5, -jnp.inf)
        tops = [row_to_column(ref[toks + b : toks + b + 1, :]) for ref in (own_ref, far_ref)]
        sums = [row_to_column(ref[toks + 4 + b : toks + 5 + b, :]) for ref in (own_ref, far_ref)]
        top = jnp.maximum(jnp.maximum(tops[0], tops[1]), jnp.max(scores, axis=1, keepdims=True))
        exps = jnp.exp(scores - top)
        mixture = nt_dot(exps.astype(jnp.bfloat16), value_ref[:, columns])
        total = jnp.sum(exps, axis=1, keepdims=True)
        for ref, peak, row_sum in zip((own_ref, far_ref), tops, sums):
            fade = jnp.exp(peak - top)
            total = total + row_sum * fade
            mixture = mixture + ref[rows, :] * fade
        out_ref[rows, :] = (mixture / total).astype(jnp.bfloat16)


def combine(own, far, query_kv, key_t, value_t):
    toks = key_t.shape[1]
    return pl.pallas_call(
        combine_kernel,
        out_shape=jax.ShapeDtypeStruct((toks, 128), jnp.bfloat16),
        in_specs=in_vmem(5),
        out_specs=in_vmem(1)[0],
        compiler_params=params(),
        cost_estimate=cost(0, 1 << 20),
        name="combine",
    )(own, far, query_kv, key_t, value_t)


def swap(values, bits):
    return lax.ppermute(values, "inst", [(i, i ^ bits) for i in range(16)])


def hop(values, step, step_count):
    pairs = []
    for i in range(16):
        plane = i // 4
        sends = plane >= step_count - 1 if step > 0 else plane <= 4 - step_count
        if sends and 0 <= plane + step <= 3:
            pairs.append((i, i + 4 * step))
    return lax.ppermute(values, "inst", pairs)


def on_16_devices(
    hidden, gain, w_query, w_key, w_value, cache_pool, prefix_len, hit_page, decode_owner
):
    me = lax.axis_index("inst")
    plane, lane = me // 4, me % 4
    toks, block = hidden.shape
    pool_dev, page_len = cache_pool.shape[0], cache_pool.shape[1]
    requests = prefix_len.shape[0]
    new_len = toks // requests
    slots = pool_dev // 2
    head = me // 8
    rows_new = decode_owner.shape[0]
    row_ids = jnp.arange(rows_new, dtype=jnp.int32)
    before_rows = (decode_owner[None, :] == decode_owner[:, None]) & (
        row_ids[None, :] < row_ids[:, None]
    )
    slot_num = jnp.sum(before_rows.astype(jnp.int32), axis=1)
    owned = (decode_owner[None, :] == me) & (
        slot_num[None, :] == jnp.arange(OWN, dtype=jnp.int32)[:, None]
    )
    pick_row = jnp.sum(jnp.where(owned, row_ids[None, :], 0), axis=1)
    has_row = jnp.any(owned, axis=1).astype(jnp.int32)
    place = jnp.stack([me, head, plane, lane]).astype(jnp.int32)
    page_place = jnp.concatenate(
        [place, jnp.full((1,), pool_dev, jnp.int32), jnp.stack([pick_row, has_row], 1).reshape(-1)]
    )
    sort_place = jnp.concatenate([place, jnp.full((1,), pool_dev, jnp.int32)])
    hits = hit_page.reshape(-1)

    wide = hidden.astype(jnp.float32)
    squares = jnp.sum(wide * wide, axis=1)
    squares = squares + swap(squares, 1)
    squares = squares + swap(squares, 2)
    squares = squares + swap(squares, 4) + (swap(squares, 8) + swap(squares, 12))
    inv = lax.rsqrt(squares / (block * 16) + EPS)[:, None]

    downs, ups = [hidden], [hidden]
    for k in (1, 2, 3):
        downs.append(hop(downs[-1], -1, k))
        ups.append(hop(ups[-1], 1, k))

    packed = pack_weights(place, w_query, w_key.T, w_value.T)
    weights = [packed[0]] + [swap(packed[r], r) for r in (1, 2, 3)]

    mine, other = pick_pages(place, hits, cache_pool, slots)
    pages = [mine, swap(other, 8)]
    pages = [pages[0], swap(pages[0], 2), pages[1], swap(pages[1], 2)]
    pages = [each for page in pages for each in (page, swap(page, 1))]
    keys, values, count = sort_pages(sort_place, hits, prefix_len, pages, page_len)

    positions = (
        jnp.repeat(prefix_len, new_len) + jnp.tile(jnp.arange(new_len, dtype=jnp.int32), requests)
    ).astype(jnp.float32)
    cos_table, sin_table = rotary_tables(positions, 128)
    cos_wide = jnp.concatenate([cos_table, cos_table], axis=1)
    sin_wide = jnp.concatenate([-sin_table, sin_table], axis=1)

    gain_blocks = lax.dynamic_index_in_dim(gain.reshape(4, 4, block), lane, 1, keepdims=False)
    gain_blocks = jnp.concatenate([gain_blocks, gain_blocks], axis=0)
    gain_blocks = lax.dynamic_slice_in_dim(gain_blocks, plane, 4, 0)
    near, far = project(place, inv, gain_blocks, hidden, downs[1:], ups[1:], weights)
    got = swap(far, 1)
    far_sum = swap(near[toks + 128 :] + got[toks + 128 :], 2)
    query_kv = finish(near, got, far_sum, cos_wide, sin_wide)

    from_plane = swap(query_kv, 4)
    kv = query_kv[toks:]
    near_kv = jnp.stack([kv, from_plane[toks:], swap(kv, 8), swap(kv, 12)])
    side_kv = swap(near_kv, 2)
    core_kv = swap(jnp.concatenate([near_kv, side_kv], axis=0), 1)

    partner_part = swap(attend(count, from_plane, keys, values, toks), 4)
    own_part = attend(count, query_kv, keys, values, toks)
    key_t, value_t, decode_pages = new_tokens(
        page_place, near_kv, side_kv, core_kv, cos_table.T, sin_table.T, page_len
    )
    attn_out = combine(own_part, partner_part, query_kv, key_t, value_t)
    return (attn_out, decode_pages)


def solution(mesh):
    return jax.shard_map(
        on_16_devices if mesh.shape["inst"] == 16 else on_device,
        mesh=mesh,
        in_specs=(
            P("groups", "inst"),
            P(),
            P(None, "inst"),
            P(None, "inst"),
            P(None, "inst"),
            P(("groups", "inst"), None, None, None),
            P("groups"),
            P("groups", None),
            P("groups"),
        ),
        out_specs=(P("groups", "inst"), P(("groups", "inst"), None, None, None)),
        check_vma=False,
    )
```

```python
import functools

import jax
import jax.numpy as jnp
from jax import lax
from jax.experimental import pallas as pl
from jax.experimental.pallas import tpu as pltpu
from jax.sharding import PartitionSpec as P

OWN = 2


EPS = 1e-05
ROPE_BASE = 500000.0


def rotary_tables(positions, head_dim):
    half_dim = head_dim // 2
    freqs = ROPE_BASE ** (-(jnp.arange(half_dim, dtype=jnp.float32) * 2.0 / head_dim))
    angles = positions[:, None] * freqs[None, :]
    return (jnp.cos(angles), jnp.sin(angles))


def rotate_rows(values, cos_table, sin_table):
    half_dim = values.shape[-1] // 2
    first_half = values[..., :half_dim]
    second_half = values[..., half_dim:]
    return jnp.concatenate(
        [
            first_half * cos_table - second_half * sin_table,
            second_half * cos_table + first_half * sin_table,
        ],
        axis=-1,
    )


def rotate_cols(values, cos_table, sin_table):
    half_dim = values.shape[-2] // 2
    first_half = values[..., :half_dim, :]
    second_half = values[..., half_dim:, :]
    return jnp.concatenate(
        [
            first_half * cos_table - second_half * sin_table,
            second_half * cos_table + first_half * sin_table,
        ],
        axis=-2,
    )


def contract_last(left, right):
    return lax.dot_general(
        left, right, (((1,), (1,)), ((), ())), preferred_element_type=jnp.float32
    )


def contract_first(weights, rows):
    return lax.dot_general(
        weights, rows, (((0,), (1,)), ((), ())), preferred_element_type=jnp.float32
    )


def on_device(
    hidden, gain, w_query, w_key, w_value, cache_pool, prefix_len, hit_page, decode_owner
):
    my_index = lax.axis_index("inst")
    devices = lax.axis_size("inst")
    tok_count = hidden.shape[0]
    head_dim = w_query.shape[1]
    requests = prefix_len.shape[0]
    new_len = tok_count // requests
    gathered = lax.all_gather(hidden, "inst", axis=1, tiled=True)
    wide_vals = gathered.astype(jnp.float32)
    inverse_rms = lax.rsqrt(jnp.mean(wide_vals * wide_vals, axis=-1, keepdims=True) + EPS)
    normed = (wide_vals * inverse_rms * gain).astype(jnp.bfloat16)
    query = jnp.dot(normed, w_query, preferred_element_type=jnp.float32)
    key_cols = contract_first(w_key, normed)
    value_cols = contract_first(w_value, normed)
    new_kv = jnp.stack([key_cols.astype(jnp.bfloat16), value_cols.astype(jnp.bfloat16)])
    all_kv = lax.all_gather(new_kv, "inst", axis=1, tiled=True)
    kv_dim = all_kv.shape[1]
    kv_heads = kv_dim // head_dim
    group_size = devices // kv_heads
    my_group = my_index // group_size
    positions = (
        jnp.repeat(prefix_len, new_len) + jnp.tile(jnp.arange(new_len, dtype=jnp.int32), requests)
    ).astype(jnp.float32)
    cos_table, sin_table = rotary_tables(positions, head_dim)
    q_rot = rotate_rows(query, cos_table, sin_table).astype(jnp.bfloat16)
    k_rot = rotate_cols(
        all_kv[0].astype(jnp.float32).reshape(kv_heads, head_dim, tok_count),
        cos_table.T,
        sin_table.T,
    ).astype(jnp.bfloat16)
    v_heads = all_kv[1].reshape(kv_heads, head_dim, tok_count)
    my_keys = lax.dynamic_index_in_dim(k_rot, my_group, 0, keepdims=False)
    my_values = lax.dynamic_index_in_dim(v_heads, my_group, 0, keepdims=False)
    pool_dev = cache_pool.shape[0]
    page_len = cache_pool.shape[1]
    hit_slots = pool_dev // 2
    flat_hits = hit_page.reshape(-1)
    entries = flat_hits.shape[0]
    is_valid = flat_hits >= 0
    holder = jnp.where(is_valid, flat_hits // pool_dev, -1)
    pool_slot = jnp.where(is_valid, flat_hits % pool_dev, 0)
    entry_ids = jnp.arange(entries, dtype=jnp.int32)
    earlier = (
        (holder[None, :] == holder[:, None])
        & (entry_ids[None, :] < entry_ids[:, None])
        & is_valid[None, :]
    )
    ranking = jnp.sum(earlier.astype(jnp.int32), axis=1)
    mine = is_valid & (holder == my_index)
    chosen = mine[None, :] & (ranking[None, :] == jnp.arange(hit_slots, dtype=jnp.int32)[:, None])
    pool_index = jnp.sum(jnp.where(chosen, pool_slot[None, :], 0), axis=1)
    present = jnp.any(chosen, axis=1)
    picked = cache_pool[pool_index]
    picked = jnp.where(present[:, None, None, None], picked, jnp.zeros_like(picked))
    inv_scale = head_dim ** (-0.5)
    per_head = picked.reshape(hit_slots, page_len, 2, kv_heads, head_dim).transpose(3, 0, 1, 2, 4)
    outgoing = jnp.repeat(per_head, group_size, axis=0)
    incoming = lax.all_to_all(outgoing, "inst", split_axis=0, concat_axis=0, tiled=True)
    stacked = incoming.reshape(devices * hit_slots, page_len, 2, head_dim)
    where_from = jnp.where(is_valid, holder * hit_slots + ranking, 0)
    prefix_rows = stacked[where_from]
    prefix_keys = prefix_rows[:, :, 0].reshape(requests, -1, head_dim)
    prefix_values = prefix_rows[:, :, 1].reshape(requests, -1, head_dim)
    prefix_span = prefix_keys.shape[1]
    causal_ok = (
        jnp.arange(new_len, dtype=jnp.int32)[None, :]
        <= jnp.arange(new_len, dtype=jnp.int32)[:, None]
    )
    pieces = []
    for request in range(requests):
        lower = request * new_len
        q_part = q_rot[lower : lower + new_len]
        pre_scores = contract_last(q_part, prefix_keys[request]) * inv_scale
        new_scores = (
            jnp.dot(q_part, my_keys[:, lower : lower + new_len], preferred_element_type=jnp.float32)
            * inv_scale
        )
        prefix_ok = jnp.arange(prefix_span, dtype=jnp.int32)[None, :] < prefix_len[request]
        row_max = jnp.maximum(
            jnp.max(jnp.where(prefix_ok, pre_scores, -jnp.inf), axis=1),
            jnp.max(jnp.where(causal_ok, new_scores, -jnp.inf), axis=1),
        )[:, None]
        pre_exps = jnp.where(prefix_ok, jnp.exp(pre_scores - row_max), 0.0)
        new_exps = jnp.where(causal_ok, jnp.exp(new_scores - row_max), 0.0)
        row_sum = jnp.sum(pre_exps, axis=1, keepdims=True) + jnp.sum(
            new_exps, axis=1, keepdims=True
        )
        mixture = jnp.dot(
            pre_exps.astype(jnp.bfloat16),
            prefix_values[request],
            preferred_element_type=jnp.float32,
        )
        mixture = mixture + contract_last(
            new_exps.astype(jnp.bfloat16), my_values[:, lower : lower + new_len]
        )
        pieces.append((mixture / row_sum).astype(jnp.bfloat16))
    attn_out = jnp.concatenate(pieces, axis=0)
    pages_new = new_len // page_len
    rows_new = decode_owner.shape[0]
    k_pages = (
        k_rot.reshape(kv_heads, head_dim, requests, pages_new, page_len)
        .transpose(2, 3, 0, 4, 1)
        .reshape(rows_new, page_len, head_dim)
    )
    v_pages = (
        v_heads.reshape(kv_heads, head_dim, requests, pages_new, page_len)
        .transpose(2, 3, 0, 4, 1)
        .reshape(rows_new, page_len, head_dim)
    )
    row_ids = jnp.arange(rows_new, dtype=jnp.int32)
    before_rows = (decode_owner[None, :] == decode_owner[:, None]) & (
        row_ids[None, :] < row_ids[:, None]
    )
    slot_num = jnp.sum(before_rows.astype(jnp.int32), axis=1)
    owned = (decode_owner[None, :] == my_index) & (
        slot_num[None, :] == jnp.arange(OWN, dtype=jnp.int32)[:, None]
    )
    pick_row = jnp.sum(jnp.where(owned, row_ids[None, :], 0), axis=1)
    has_row = jnp.any(owned, axis=1)
    page_pair = jnp.stack([k_pages[pick_row], v_pages[pick_row]], axis=2)
    decode_pages = jnp.where(has_row[:, None, None, None], page_pair, jnp.zeros_like(page_pair))
    return (attn_out, decode_pages)


VMEM_LIMIT = 48 * 1024 * 1024
CHUNK = 512
SUM_ROWS = 16


def in_vmem(count):
    return [pl.BlockSpec(memory_space=pltpu.VMEM)] * count


def in_smem(count):
    return [pl.BlockSpec(memory_space=pltpu.SMEM)] * count


def params():
    return pltpu.CompilerParams(vmem_limit_bytes=VMEM_LIMIT)


def cost(flops, nbytes):
    return pl.CostEstimate(flops=flops, bytes_accessed=nbytes, transcendentals=0)


def nt_dot(left, right):
    return lax.dot_general(
        left, right, (((1,), (1,)), ((), ())), preferred_element_type=jnp.float32
    )


def holder_of(page, pool_dev):
    if pool_dev & (pool_dev - 1) == 0:
        return jnp.right_shift(page, pool_dev.bit_length() - 1)
    return page // pool_dev


def pick_pages_kernel(place_ref, hits_ref, pool_ref, mine_ref, other_ref, held, sems):
    me, head = place_ref[0], place_ref[1]
    pool_dev, page_len = pool_ref.shape[0], pool_ref.shape[1]
    slots = held.shape[0]
    rows = 2 * page_len
    out_row = lax.broadcasted_iota(jnp.int32, (rows, rows), 0)
    in_row = lax.broadcasted_iota(jnp.int32, (rows, rows), 1)
    wanted = jnp.where(out_row < page_len, 2 * out_row, 2 * (out_row - page_len) + 1)
    unweave = (in_row == wanted).astype(jnp.bfloat16)

    def fetch(page, slot):
        return pltpu.make_async_copy(pool_ref.at[page], held.at[slot], sems.at[slot])

    def entry(e, count):
        page = hits_ref[e]
        is_mine = (page >= 0) & (holder_of(page, pool_dev) == me)

        @pl.when(is_mine)
        def _():
            fetch(page - me * pool_dev, count).start()

        return count + is_mine.astype(jnp.int32)

    count = lax.fori_loop(0, hits_ref.shape[0], entry, jnp.int32(0))

    def arrive(slot, carry):
        fetch(0, slot).wait()
        return carry

    lax.fori_loop(0, count, arrive, 0)
    for slot in range(slots):
        at = slice(slot * rows, (slot + 1) * rows)
        slab = held[slot]
        first = slab[:, :, :128].reshape(rows, 128)
        second = slab[:, :, 128:].reshape(rows, 128)
        both = jnp.concatenate([first, second], axis=1)
        both = jnp.dot(unweave, both, preferred_element_type=jnp.float32)
        both = both.astype(jnp.bfloat16)
        mine_ref[at, :] = jnp.where(head == 0, both[:, :128], both[:, 128:])
        other_ref[at, :] = jnp.where(head == 0, both[:, 128:], both[:, :128])


def pick_pages(place, hits, pool, slots):
    rows = slots * 2 * pool.shape[1]
    block = jax.ShapeDtypeStruct((rows, 128), jnp.bfloat16)
    return pl.pallas_call(
        pick_pages_kernel,
        out_shape=(block, block),
        in_specs=in_smem(2) + [pl.BlockSpec(memory_space=pl.ANY)],
        out_specs=tuple(in_vmem(2)),
        scratch_shapes=[
            pltpu.VMEM((slots,) + pool.shape[1:], jnp.bfloat16),
            pltpu.SemaphoreType.DMA((slots,)),
        ],
        compiler_params=params(),
        cost_estimate=cost(0, 4 * pool.size),
        name="pick_pages",
    )(place, hits, pool)


def column_to_row(column):
    return jnp.transpose(jnp.broadcast_to(column, (128, 128)))[0:1]


def row_to_column(row):
    return jnp.transpose(jnp.broadcast_to(row, (128, 128)))[:, 0:1]


def plane_order(plane):
    return [0, jnp.where(plane <= 2, 1, 3), 2, jnp.where(plane <= 2, 3, 1)]


def pack_weights_kernel(place_ref, wq_ref, wk_ref, wv_ref, *refs):
    own_ref, core_ref, side_ref, wk, wv, sems = refs
    plane, lane = place_ref[2], place_ref[3]
    feats = wk.shape[0]
    block = wq_ref.shape[0] // 16
    half = own_ref.shape[0]
    parts = []
    for r, out_ref in enumerate((own_ref, core_ref, side_ref, side_ref)):
        for k, offset in enumerate(plane_order(plane)):
            start = (((plane + offset) & 3) * 4 + (lane ^ r)) * block
            base = half if r == 3 else 0
            parts.append((out_ref, base, k, pl.multiple_of(start, block)))
    copies = [
        pltpu.make_async_copy(
            wq_ref.at[pl.ds(start, block)],
            out_ref.at[pl.ds(base + k * block, block)],
            sems.at[n],
        )
        for n, (out_ref, base, k, start) in enumerate(parts)
    ]
    copies.append(pltpu.make_async_copy(wk_ref, wk, sems.at[16]))
    copies.append(pltpu.make_async_copy(wv_ref, wv, sems.at[17]))
    for copy in copies[16:] + copies[:16]:
        copy.start()
    for copy in copies[16:]:
        copy.wait()
    for out_ref, base, k, start in parts:
        for j in range(block // 128):
            at = base + 4 * block + (k * (block // 128) + j) * 2 * feats
            columns = pl.ds(pl.multiple_of(start + j * 128, 128), 128)
            out_ref[at : at + feats, :] = wk[:, columns]
            out_ref[at + feats : at + 2 * feats, :] = wv[:, columns]
    for copy in copies[:16]:
        copy.wait()


def pack_weights(place, wq, wk_t, wv_t):
    rows = wq.shape[0] // 4 + 2 * wk_t.shape[0] * wk_t.shape[1] // 4 // 128
    block = jax.ShapeDtypeStruct((rows, 128), jnp.bfloat16)
    return pl.pallas_call(
        pack_weights_kernel,
        out_shape=(block, block, jax.ShapeDtypeStruct((2 * rows, 128), jnp.bfloat16)),
        in_specs=in_smem(1) + [pl.BlockSpec(memory_space=pl.ANY)] * 3,
        out_specs=tuple(in_vmem(3)),
        scratch_shapes=[
            pltpu.VMEM(wk_t.shape, jnp.bfloat16),
            pltpu.VMEM(wv_t.shape, jnp.bfloat16),
            pltpu.SemaphoreType.DMA((18,)),
        ],
        compiler_params=params(),
        cost_estimate=cost(0, 2 * wq.size),
        name="pack_weights",
    )(place, wq, wk_t, wv_t)


def project_block(k, raw, inv, gain_ref, weights, block):
    chunks = block // 128
    normed = (raw.astype(jnp.float32) * inv * gain_ref[k : k + 1, :]).astype(jnp.bfloat16)
    wide = jnp.concatenate([ref[k * block : (k + 1) * block, :] for ref in weights], axis=1)
    kv_rows = []
    for ref in weights:
        pieces = []
        for j in range(chunks):
            at = 4 * block + (k * chunks + j) * 32
            pieces.append(ref[at : at + 32, :])
        kv_rows.append(jnp.concatenate(pieces, axis=1))
    parts = jnp.dot(normed, wide, preferred_element_type=jnp.float32)
    return parts, nt_dot(jnp.concatenate(kv_rows, axis=0), normed)


def add_sums_kernel(hidden_ref, squares_ref, out_ref):
    toks = hidden_ref.shape[0]
    out_ref[:toks, :] = hidden_ref[...]
    left = squares_ref[...]
    rows = []
    for _ in range(3):
        rows.append(left.astype(jnp.bfloat16).astype(jnp.float32))
        left = left - rows[-1]
    rows.append(jnp.zeros((SUM_ROWS - 3, toks), jnp.float32))
    out_ref[toks:, :] = jnp.concatenate(rows, axis=0).astype(jnp.bfloat16)


def add_sums(hidden, squares):
    toks, block = hidden.shape
    return pl.pallas_call(
        add_sums_kernel,
        out_shape=jax.ShapeDtypeStruct((toks + SUM_ROWS, block), jnp.bfloat16),
        in_specs=in_vmem(2),
        out_specs=in_vmem(1)[0],
        compiler_params=params(),
        cost_estimate=cost(0, 1 << 20),
        name="add_sums",
    )(hidden, squares.reshape(1, toks))


def project_kernel(place_ref, gain_ref, own_ref, *refs):
    downs, ups, weights, out_refs = refs[0:3], refs[3:6], refs[6:10], refs[10:]
    plane = place_ref[2]
    block = own_ref.shape[1]
    toks = own_ref.shape[0] - SUM_ROWS
    sources = (
        lambda at: own_ref[at],
        lambda at: jnp.where(plane <= 2, downs[0][at], ups[0][at]),
        lambda at: jnp.where(plane <= 1, downs[1][at], ups[1][at]),
        lambda at: jnp.where(
            plane == 0, downs[2][at], jnp.where(plane == 3, ups[2][at], ups[0][at])
        ),
    )
    squares = sum(
        jnp.sum(source(slice(toks, toks + SUM_ROWS)).astype(jnp.float32), axis=0, keepdims=True)
        for source in sources
    )
    inv = lax.rsqrt(squares / (block * 16) + EPS)
    inv = jnp.concatenate(
        [row_to_column(inv[:, t : t + 128]) for t in range(0, toks, 128)], axis=0
    )
    query, kv_total = None, None
    for k, source in enumerate(sources):
        parts, kv_part = project_block(k, source(slice(0, toks)), inv, gain_ref, weights, block)
        query = parts if k == 0 else query + parts
        kv_total = kv_part if k == 0 else kv_total + kv_part
    half = toks // 2
    for n, out_ref in enumerate(out_refs):
        r, rows = n // 2, slice(n % 2 * half, (n % 2 + 1) * half)
        out_ref[:half, :] = query[rows, r * 128 : (r + 1) * 128]
        for t in range(half // 128):
            chunk = slice(rows.start + t * 128, rows.start + (t + 1) * 128)
            out_ref[half + t * 32 : half + (t + 1) * 32, :] = kv_total[r * 32 : (r + 1) * 32, chunk]


def project(place, gain, downs, ups, weights):
    toks = downs[0].shape[0] - SUM_ROWS
    out = jax.ShapeDtypeStruct(((toks + 128) // 2, 128), jnp.float32)
    return pl.pallas_call(
        project_kernel,
        out_shape=(out,) * 8,
        in_specs=in_smem(1) + in_vmem(12),
        out_specs=tuple(in_vmem(8)),
        compiler_params=params(),
        cost_estimate=cost(2 * toks * 512 * 640, 6 << 20),
        name="project",
    )(place, gain, *downs, *ups[1:], *weights)


def finish_kernel(*refs):
    cos_ref, sin_ref, out_ref = refs[6:]
    toks = cos_ref.shape[0]
    half, kv_rows = toks // 2, 64
    for n in range(2):
        rows = slice(n * half, (n + 1) * half)
        total = refs[n][...] + refs[2 + n][...] + refs[4 + n][...]
        query = total[:half]
        swapped = jnp.concatenate([query[:, 64:], query[:, :64]], axis=1)
        rotated = query * cos_ref[rows, :] + swapped * sin_ref[rows, :]
        out_ref[rows, :] = rotated.astype(jnp.bfloat16)
        at = toks + n * kv_rows
        out_ref[at : at + kv_rows, :] = total[half:].astype(jnp.bfloat16)


def finish(own, got, far_sum, cos_wide, sin_wide):
    toks = cos_wide.shape[0]
    return pl.pallas_call(
        finish_kernel,
        out_shape=jax.ShapeDtypeStruct((toks + 128, 128), jnp.bfloat16),
        in_specs=in_vmem(8),
        out_specs=in_vmem(1)[0],
        compiler_params=params(),
        cost_estimate=cost(0, 2 << 20),
        name="finish_projection",
    )(*own, *got, *far_sum, cos_wide, sin_wide)


def lane_tiles(values, join):
    joined = values[:, :128]
    for start in range(128, values.shape[1], 128):
        joined = join(joined, values[:, start : start + 128])
    return joined


def put_state(out_ref, toks, first, acc, top, total):
    out_ref[first : first + acc.shape[0], :] = acc
    for b in range(acc.shape[0] // 128):
        row, part = toks + first // 128 + b, slice(b * 128, (b + 1) * 128)
        out_ref[row : row + 1, :] = column_to_row(top[part])
        out_ref[row + 4 : row + 5, :] = column_to_row(total[part])


def get_state(ref, toks, first, count):
    rows = range(toks + first // 128, toks + (first + count) // 128)
    top = [row_to_column(ref[row : row + 1, :]) for row in rows]
    total = [row_to_column(ref[row + 4 : row + 5, :]) for row in rows]
    return ref[first : first + count, :], jnp.concatenate(top), jnp.concatenate(total)


def merge_states(states):
    peak = functools.reduce(jnp.maximum, [top for _, top, _ in states])
    base = jnp.where(peak == -jnp.inf, 0.0, peak)
    fades = [jnp.exp(top - base) for _, top, _ in states]
    acc = sum(acc * fade for (acc, _, _), fade in zip(states, fades))
    total = sum(total * fade for (_, _, total), fade in zip(states, fades))
    return acc, peak, total


def attend_kernel(offset, page_len, earlier, table_ref, *refs):
    blocks, (own_ref, far_ref), refs = refs[:4], refs[4:6], refs[6:]
    before = refs[:2] if earlier else ()
    outs, (held, keys, values, scores_ref, acc, lanes, sems) = refs[-9:-7], refs[-7:]
    copies = [
        pltpu.make_async_copy(block, held.at[n], sems.at[n]) for n, block in enumerate(blocks)
    ]
    for copy in copies:
        copy.start()
    me = table_ref[0] ^ offset
    toks = outs[0].shape[0] - 8
    new_len = toks // 2
    chunk_pages = CHUNK // page_len
    for copy in copies:
        copy.wait()
    for request in range(2):
        last_holder = table_ref[1 + request]
        has_last = (last_holder & 12) == (me & 12)
        pages = jnp.int32(0)
        for n in range(4):
            holder = (me & 12) | ((last_holder + 1 + n) & 3)
            count = table_ref[5 + request * 16 + holder]
            first = table_ref[5 + holder] if request else jnp.int32(0)
            which = (holder ^ me) & 3

            def move(p, carry, which=which, first=first, pages=pages):
                source = pl.multiple_of((first + p) * 2 * page_len, 2 * page_len)
                target = pl.multiple_of((pages + p) * page_len, page_len)
                keys[pl.ds(target, page_len), :] = held[which, pl.ds(source, page_len), :]
                values[pl.ds(target, page_len), :] = held[
                    which, pl.ds(source + page_len, page_len), :
                ]
                return carry

            lax.fori_loop(0, count, move, 0)
            pages = pages + count
        trips = (pages + chunk_pages - 1) // chunk_pages

        def clear(p, carry):
            target = pl.multiple_of(p * page_len, page_len)
            values[pl.ds(target, page_len), :] = jnp.zeros((page_len, 128), jnp.bfloat16)
            return carry

        lax.fori_loop(pages, trips * chunk_pages, clear, 0)
        keys_here = pages * page_len - jnp.where(has_last, table_ref[3 + request], 0)
        rows = slice(request * new_len, (request + 1) * new_len)
        query = jnp.concatenate([far_ref[rows, :], own_ref[rows, :]], axis=0)
        lanes[...] = jnp.full_like(lanes, -jnp.inf)

        def score(n, carry, query=query, keys_here=keys_here):
            at = pl.ds(pl.multiple_of(n * CHUNK, CHUNK), CHUNK)
            scores = nt_dot(query, keys[at, :]) * 128**-0.5
            column = lax.broadcasted_iota(jnp.int32, scores.shape, 1)
            scores = jnp.where(column < keys_here - n * CHUNK, scores, -jnp.inf)
            scores_ref[:, at] = scores
            lanes[...] = jnp.maximum(lanes[...], lane_tiles(scores, jnp.maximum))
            return carry

        lax.fori_loop(0, trips, score, 0)
        top = jnp.max(lanes[...], axis=1, keepdims=True)
        lanes[...] = jnp.zeros_like(lanes)
        acc[...] = jnp.zeros_like(acc)

        def mix(n, carry, top=top):
            at = pl.ds(pl.multiple_of(n * CHUNK, CHUNK), CHUNK)
            exps = jnp.exp(scores_ref[:, at] - top)
            lanes[...] += lane_tiles(exps, jnp.add)
            acc[...] += jnp.dot(
                exps.astype(jnp.bfloat16), values[at, :], preferred_element_type=jnp.float32
            )
            return carry

        lax.fori_loop(0, trips, mix, 0)
        total = jnp.sum(lanes[...], axis=1, keepdims=True)
        for n, out_ref in enumerate(outs):
            part = slice(n * new_len, (n + 1) * new_len)
            state = (acc[part, :], top[part], total[part])
            if earlier:
                past = get_state(before[n], toks, request * new_len, new_len)
                state = merge_states([past, state])
            put_state(out_ref, toks, request * new_len, *state)


def attend(offset, table, blocks, own_query, far_query, earlier, toks, span, page_len):
    new_len = toks // 2
    state = jax.ShapeDtypeStruct((toks + 8, 128), jnp.float32)
    return pl.pallas_call(
        functools.partial(attend_kernel, offset, page_len, bool(earlier)),
        out_shape=(state, state),
        in_specs=in_smem(1)
        + [pl.BlockSpec(memory_space=pl.ANY)] * 4
        + in_vmem(2 + len(earlier)),
        out_specs=tuple(in_vmem(2)),
        scratch_shapes=[
            pltpu.VMEM((4,) + blocks[0].shape, jnp.bfloat16),
            pltpu.VMEM((span, 128), jnp.bfloat16),
            pltpu.VMEM((span, 128), jnp.bfloat16),
            pltpu.VMEM((toks, span), jnp.float32),
            pltpu.VMEM((toks, 128), jnp.float32),
            pltpu.VMEM((toks, 128), jnp.float32),
            pltpu.SemaphoreType.DMA((4,)),
        ],
        compiler_params=params(),
        cost_estimate=cost(1, 20 << 20),
        name="attend_far_plane" if offset else "attend_own_plane",
    )(table, *blocks, own_query, far_query, *earlier)


def new_tokens_kernel(
    place_ref, near_ref, side_ref, core_ref, cos_ref, sin_ref, query_ref, state_ref, page_ref, held, kt, vt
):
    me, head = place_ref[0], place_ref[1]
    toks = cos_ref.shape[1]
    for n in range(4):
        held[n] = near_ref[n]
        held[4 + n] = side_ref[n]
    for n in range(8):
        held[8 + n] = core_ref[n]
    for device in range(16):
        rel = device ^ me
        block = held[(rel & 1) * 8 + ((rel >> 1) & 1) * 4 + (rel >> 2)]
        rows = slice((device % 8) * 16, (device % 8) * 16 + 16)
        for t in range(toks // 128):
            columns = slice(t * 128, (t + 1) * 128)
            kt[device // 8, rows, columns] = block[t * 32 : t * 32 + 16]
            vt[device // 8, rows, columns] = block[t * 32 + 16 : t * 32 + 32]
    cos, sin = cos_ref[...], sin_ref[...]
    for g in range(2):
        first = kt[g, :64, :].astype(jnp.float32)
        second = kt[g, 64:, :].astype(jnp.float32)
        kt[g, :64, :] = (first * cos - second * sin).astype(jnp.bfloat16)
        kt[g, 64:, :] = (second * cos + first * sin).astype(jnp.bfloat16)
    new_len = toks // 2
    query_at = lax.broadcasted_iota(jnp.int32, (new_len, new_len), 0)
    key_at = lax.broadcasted_iota(jnp.int32, (new_len, new_len), 1)
    for request in range(2):
        part = slice(request * new_len, (request + 1) * new_len)
        scores = jnp.dot(
            query_ref[part, :], kt[head, :, part], preferred_element_type=jnp.float32
        )
        scores = jnp.where(key_at <= query_at, scores * 128**-0.5, -jnp.inf)
        top = jnp.max(scores, axis=1, keepdims=True)
        exps = jnp.exp(scores - top)
        acc = nt_dot(exps.astype(jnp.bfloat16), vt[head, :, part])
        total = jnp.sum(exps, axis=1, keepdims=True)
        put_state(state_ref, toks, request * new_len, acc, top, total)
    page_len = page_ref.shape[1]
    out_row = lax.broadcasted_iota(jnp.int32, (2 * page_len, 128), 0)
    token = lax.broadcasted_iota(jnp.int32, (2 * page_len, 128), 1)
    for slot in range(page_ref.shape[0]):
        row, has = place_ref[4 + 2 * slot], place_ref[5 + 2 * slot]
        start = (row // 8) * (toks // 2) + ((row // 2) % 4) * page_len
        columns = pl.ds(pl.multiple_of(start // 128 * 128, 128), 128)
        inside = token - start % 128
        inside = jnp.where(has > 0, inside, -1)
        take_k = ((out_row % 2 == 0) & (inside == out_row // 2)).astype(jnp.bfloat16)
        take_v = ((out_row % 2 == 1) & (inside == out_row // 2)).astype(jnp.bfloat16)
        woven = nt_dot(take_k, kt[row % 2, :, columns]) + nt_dot(take_v, vt[row % 2, :, columns])
        page_ref[slot] = woven.astype(jnp.bfloat16).reshape(page_len, 2, 128)


def new_tokens(place, near, side, core, cos_t, sin_t, query_kv, page_len):
    toks = cos_t.shape[1]
    return pl.pallas_call(
        new_tokens_kernel,
        out_shape=(
            jax.ShapeDtypeStruct((toks + 8, 128), jnp.float32),
            jax.ShapeDtypeStruct((OWN, page_len, 2, 128), jnp.bfloat16),
        ),
        in_specs=in_smem(1) + in_vmem(6),
        out_specs=tuple(in_vmem(2)),
        scratch_shapes=[
            pltpu.VMEM((16, 128, 128), jnp.bfloat16),
            pltpu.VMEM((2, 128, toks), jnp.bfloat16),
            pltpu.VMEM((2, 128, toks), jnp.bfloat16),
        ],
        compiler_params=params(),
        cost_estimate=cost(0, 2 << 20),
        name="new_tokens",
    )(place, near, side, core, cos_t, sin_t, query_kv)


def combine_kernel(own_ref, far_ref, new_ref, out_ref):
    toks = out_ref.shape[0]
    for first in range(0, toks, 128):
        states = [get_state(ref, toks, first, 128) for ref in (own_ref, far_ref, new_ref)]
        acc, _, total = merge_states(states)
        out_ref[first : first + 128, :] = (acc / total).astype(jnp.bfloat16)


def combine(own, far, new):
    toks = own.shape[0] - 8
    return pl.pallas_call(
        combine_kernel,
        out_shape=jax.ShapeDtypeStruct((toks, 128), jnp.bfloat16),
        in_specs=in_vmem(3),
        out_specs=in_vmem(1)[0],
        compiler_params=params(),
        cost_estimate=cost(0, 1 << 20),
        name="combine",
    )(own, far, new)


def swap(values, bits):
    return lax.ppermute(values, "inst", [(i, i ^ bits) for i in range(16)])


def after(values, *others):
    return lax.optimization_barrier((values, others))[0]


def hop(values, step, step_count):
    pairs = []
    for i in range(16):
        plane = i // 4
        sends = plane >= step_count - 1 if step > 0 else plane <= 4 - step_count
        if sends and 0 <= plane + step <= 3:
            pairs.append((i, i + 4 * step))
    return lax.ppermute(values, "inst", pairs)


def on_16_devices(
    hidden, gain, w_query, w_key, w_value, cache_pool, prefix_len, hit_page, decode_owner
):
    me = lax.axis_index("inst")
    plane, lane = me // 4, me % 4
    toks, block = hidden.shape
    pool_dev, page_len = cache_pool.shape[0], cache_pool.shape[1]
    requests = prefix_len.shape[0]
    new_len = toks // requests
    slots = pool_dev // 2
    head = me // 8
    rows_new = decode_owner.shape[0]
    row_ids = jnp.arange(rows_new, dtype=jnp.int32)
    before_rows = (decode_owner[None, :] == decode_owner[:, None]) & (
        row_ids[None, :] < row_ids[:, None]
    )
    slot_num = jnp.sum(before_rows.astype(jnp.int32), axis=1)
    owned = (decode_owner[None, :] == me) & (
        slot_num[None, :] == jnp.arange(OWN, dtype=jnp.int32)[:, None]
    )
    pick_row = jnp.sum(jnp.where(owned, row_ids[None, :], 0), axis=1)
    has_row = jnp.any(owned, axis=1).astype(jnp.int32)
    place = jnp.stack([me, head, plane, lane]).astype(jnp.int32)
    page_place = jnp.concatenate([place, jnp.stack([pick_row, has_row], 1).reshape(-1)])
    hits = hit_page.reshape(-1)

    holders = jnp.where(hit_page >= 0, hit_page // pool_dev, -1)
    counts = jnp.sum(
        (holders[:, :, None] == jnp.arange(16, dtype=jnp.int32)).astype(jnp.int32), axis=1
    )
    last_page = (prefix_len - 1) // page_len
    is_last = jnp.arange(hit_page.shape[1], dtype=jnp.int32)[None, :] == last_page[:, None]
    last_holder = jnp.sum(jnp.where(is_last, holders, 0), axis=1)
    missing = (last_page + 1) * page_len - prefix_len
    table = jnp.concatenate([me[None], last_holder, missing, counts.reshape(-1)]).astype(jnp.int32)

    wide = hidden.astype(jnp.float32)
    squares = jnp.sum(wide * wide, axis=1)
    for bit in (1, 2):
        squares = squares + swap(squares, bit)

    w_own, w_core, w_side = pack_weights(place, w_query, w_key.T, w_value.T)
    w_side = swap(after(w_side, squares), 2)
    rows = w_own.shape[0]
    weights = [w_own, swap(w_core, 1), w_side, swap(w_side[rows:], 1)]

    mine, other = pick_pages(place, hits, cache_pool, slots)
    first = add_sums(hidden, squares)
    downs, ups = [first], [first]
    for k in (1, 2, 3):
        down, up = downs[-1], ups[-1]
        if k == 2:
            down, up = after((down, up), mine)
        downs.append(hop(down, -1, k))
        ups.append(hop(up, 1, k))

    mine_side = swap(after(mine, w_side), 2)
    far_pages = swap(after(other, downs[2], ups[2]), 8)

    positions = (
        jnp.repeat(prefix_len, new_len) + jnp.tile(jnp.arange(new_len, dtype=jnp.int32), requests)
    ).astype(jnp.float32)
    cos_table, sin_table = rotary_tables(positions, 128)
    cos_wide = jnp.concatenate([cos_table, cos_table], axis=1)
    sin_wide = jnp.concatenate([-sin_table, sin_table], axis=1)

    gain_blocks = lax.dynamic_index_in_dim(gain.reshape(4, 4, block), lane, 1, keepdims=False)
    gain_blocks = gain_blocks[(plane + jnp.stack(plane_order(plane))) & 3]
    sums = project(place, gain_blocks, downs, ups, weights)
    got = [swap(part, 1) for part in sums[2:4] + sums[6:8]]
    far_sum = [swap(sums[4 + n] + got[2 + n], 2) for n in range(2)]
    far_sum = after(far_sum, far_pages)
    query_kv = finish(sums[:2], got[:2], far_sum, cos_wide, sin_wide)

    far_side = swap(after(far_pages, far_sum), 2)
    near_pages = [mine, swap(mine, 1), mine_side, swap(mine_side, 1)]
    away_pages = [far_pages, swap(far_pages, 1), far_side, swap(far_side, 1)]

    from_plane = swap(query_kv, 4)
    kv = query_kv[toks:]
    far_kv = (swap(kv, 8), swap(kv, 12))

    span = hit_page.shape[1] * page_len
    sizes = (toks, span, page_len)
    part = attend(0, table, near_pages, query_kv, from_plane, (), *sizes)
    far_kv = after(far_kv, part)
    near_kv = jnp.stack([kv, from_plane[toks:], *far_kv])
    side_kv = swap(near_kv, 2)
    core_kv = swap(jnp.concatenate([near_kv, side_kv], axis=0), 1)
    partner_part, own_part = attend(8, table, away_pages, query_kv, from_plane, part, *sizes)
    partner_part = swap(partner_part, 4)
    new_part, decode_pages = new_tokens(
        page_place, near_kv, side_kv, core_kv, cos_table.T, sin_table.T, query_kv, page_len
    )
    attn_out = combine(own_part, partner_part, new_part)
    return (attn_out, decode_pages)


def solution(mesh):
    return jax.shard_map(
        on_16_devices if mesh.shape["inst"] == 16 else on_device,
        mesh=mesh,
        in_specs=(
            P("groups", "inst"),
            P(),
            P(None, "inst"),
            P(None, "inst"),
            P(None, "inst"),
            P(("groups", "inst"), None, None, None),
            P("groups"),
            P("groups", None),
            P("groups"),
        ),
        out_specs=(P("groups", "inst"), P(("groups", "inst"), None, None, None)),
        check_vma=False,
    )
```

```python
import functools

import jax
import jax.numpy as jnp
from jax import lax
from jax.experimental import pallas as pl
from jax.experimental.pallas import tpu as pltpu
from jax.sharding import PartitionSpec as P

OWN = 2


EPS = 1e-05
ROPE_BASE = 500000.0


def rotary_tables(positions, head_dim):
    half_dim = head_dim // 2
    freqs = ROPE_BASE ** (-(jnp.arange(half_dim, dtype=jnp.float32) * 2.0 / head_dim))
    angles = positions[:, None] * freqs[None, :]
    return (jnp.cos(angles), jnp.sin(angles))


def rotate_rows(values, cos_table, sin_table):
    half_dim = values.shape[-1] // 2
    first_half = values[..., :half_dim]
    second_half = values[..., half_dim:]
    return jnp.concatenate(
        [
            first_half * cos_table - second_half * sin_table,
            second_half * cos_table + first_half * sin_table,
        ],
        axis=-1,
    )


def rotate_cols(values, cos_table, sin_table):
    half_dim = values.shape[-2] // 2
    first_half = values[..., :half_dim, :]
    second_half = values[..., half_dim:, :]
    return jnp.concatenate(
        [
            first_half * cos_table - second_half * sin_table,
            second_half * cos_table + first_half * sin_table,
        ],
        axis=-2,
    )


def contract_last(left, right):
    return lax.dot_general(
        left, right, (((1,), (1,)), ((), ())), preferred_element_type=jnp.float32
    )


def contract_first(weights, rows):
    return lax.dot_general(
        weights, rows, (((0,), (1,)), ((), ())), preferred_element_type=jnp.float32
    )


def on_device(
    hidden, gain, w_query, w_key, w_value, cache_pool, prefix_len, hit_page, decode_owner
):
    my_index = lax.axis_index("inst")
    devices = lax.axis_size("inst")
    tok_count = hidden.shape[0]
    head_dim = w_query.shape[1]
    requests = prefix_len.shape[0]
    new_len = tok_count // requests
    gathered = lax.all_gather(hidden, "inst", axis=1, tiled=True)
    wide_vals = gathered.astype(jnp.float32)
    inverse_rms = lax.rsqrt(jnp.mean(wide_vals * wide_vals, axis=-1, keepdims=True) + EPS)
    normed = (wide_vals * inverse_rms * gain).astype(jnp.bfloat16)
    query = jnp.dot(normed, w_query, preferred_element_type=jnp.float32)
    key_cols = contract_first(w_key, normed)
    value_cols = contract_first(w_value, normed)
    new_kv = jnp.stack([key_cols.astype(jnp.bfloat16), value_cols.astype(jnp.bfloat16)])
    all_kv = lax.all_gather(new_kv, "inst", axis=1, tiled=True)
    kv_dim = all_kv.shape[1]
    kv_heads = kv_dim // head_dim
    group_size = devices // kv_heads
    my_group = my_index // group_size
    positions = (
        jnp.repeat(prefix_len, new_len) + jnp.tile(jnp.arange(new_len, dtype=jnp.int32), requests)
    ).astype(jnp.float32)
    cos_table, sin_table = rotary_tables(positions, head_dim)
    q_rot = rotate_rows(query, cos_table, sin_table).astype(jnp.bfloat16)
    k_rot = rotate_cols(
        all_kv[0].astype(jnp.float32).reshape(kv_heads, head_dim, tok_count),
        cos_table.T,
        sin_table.T,
    ).astype(jnp.bfloat16)
    v_heads = all_kv[1].reshape(kv_heads, head_dim, tok_count)
    my_keys = lax.dynamic_index_in_dim(k_rot, my_group, 0, keepdims=False)
    my_values = lax.dynamic_index_in_dim(v_heads, my_group, 0, keepdims=False)
    pool_dev = cache_pool.shape[0]
    page_len = cache_pool.shape[1]
    hit_slots = pool_dev // 2
    flat_hits = hit_page.reshape(-1)
    entries = flat_hits.shape[0]
    is_valid = flat_hits >= 0
    holder = jnp.where(is_valid, flat_hits // pool_dev, -1)
    pool_slot = jnp.where(is_valid, flat_hits % pool_dev, 0)
    entry_ids = jnp.arange(entries, dtype=jnp.int32)
    earlier = (
        (holder[None, :] == holder[:, None])
        & (entry_ids[None, :] < entry_ids[:, None])
        & is_valid[None, :]
    )
    ranking = jnp.sum(earlier.astype(jnp.int32), axis=1)
    mine = is_valid & (holder == my_index)
    chosen = mine[None, :] & (ranking[None, :] == jnp.arange(hit_slots, dtype=jnp.int32)[:, None])
    pool_index = jnp.sum(jnp.where(chosen, pool_slot[None, :], 0), axis=1)
    present = jnp.any(chosen, axis=1)
    picked = cache_pool[pool_index]
    picked = jnp.where(present[:, None, None, None], picked, jnp.zeros_like(picked))
    inv_scale = head_dim ** (-0.5)
    per_head = picked.reshape(hit_slots, page_len, 2, kv_heads, head_dim).transpose(3, 0, 1, 2, 4)
    outgoing = jnp.repeat(per_head, group_size, axis=0)
    incoming = lax.all_to_all(outgoing, "inst", split_axis=0, concat_axis=0, tiled=True)
    stacked = incoming.reshape(devices * hit_slots, page_len, 2, head_dim)
    where_from = jnp.where(is_valid, holder * hit_slots + ranking, 0)
    prefix_rows = stacked[where_from]
    prefix_keys = prefix_rows[:, :, 0].reshape(requests, -1, head_dim)
    prefix_values = prefix_rows[:, :, 1].reshape(requests, -1, head_dim)
    prefix_span = prefix_keys.shape[1]
    causal_ok = (
        jnp.arange(new_len, dtype=jnp.int32)[None, :]
        <= jnp.arange(new_len, dtype=jnp.int32)[:, None]
    )
    pieces = []
    for request in range(requests):
        lower = request * new_len
        q_part = q_rot[lower : lower + new_len]
        pre_scores = contract_last(q_part, prefix_keys[request]) * inv_scale
        new_scores = (
            jnp.dot(q_part, my_keys[:, lower : lower + new_len], preferred_element_type=jnp.float32)
            * inv_scale
        )
        prefix_ok = jnp.arange(prefix_span, dtype=jnp.int32)[None, :] < prefix_len[request]
        row_max = jnp.maximum(
            jnp.max(jnp.where(prefix_ok, pre_scores, -jnp.inf), axis=1),
            jnp.max(jnp.where(causal_ok, new_scores, -jnp.inf), axis=1),
        )[:, None]
        pre_exps = jnp.where(prefix_ok, jnp.exp(pre_scores - row_max), 0.0)
        new_exps = jnp.where(causal_ok, jnp.exp(new_scores - row_max), 0.0)
        row_sum = jnp.sum(pre_exps, axis=1, keepdims=True) + jnp.sum(
            new_exps, axis=1, keepdims=True
        )
        mixture = jnp.dot(
            pre_exps.astype(jnp.bfloat16),
            prefix_values[request],
            preferred_element_type=jnp.float32,
        )
        mixture = mixture + contract_last(
            new_exps.astype(jnp.bfloat16), my_values[:, lower : lower + new_len]
        )
        pieces.append((mixture / row_sum).astype(jnp.bfloat16))
    attn_out = jnp.concatenate(pieces, axis=0)
    pages_new = new_len // page_len
    rows_new = decode_owner.shape[0]
    k_pages = (
        k_rot.reshape(kv_heads, head_dim, requests, pages_new, page_len)
        .transpose(2, 3, 0, 4, 1)
        .reshape(rows_new, page_len, head_dim)
    )
    v_pages = (
        v_heads.reshape(kv_heads, head_dim, requests, pages_new, page_len)
        .transpose(2, 3, 0, 4, 1)
        .reshape(rows_new, page_len, head_dim)
    )
    row_ids = jnp.arange(rows_new, dtype=jnp.int32)
    before_rows = (decode_owner[None, :] == decode_owner[:, None]) & (
        row_ids[None, :] < row_ids[:, None]
    )
    slot_num = jnp.sum(before_rows.astype(jnp.int32), axis=1)
    owned = (decode_owner[None, :] == my_index) & (
        slot_num[None, :] == jnp.arange(OWN, dtype=jnp.int32)[:, None]
    )
    pick_row = jnp.sum(jnp.where(owned, row_ids[None, :], 0), axis=1)
    has_row = jnp.any(owned, axis=1)
    page_pair = jnp.stack([k_pages[pick_row], v_pages[pick_row]], axis=2)
    decode_pages = jnp.where(has_row[:, None, None, None], page_pair, jnp.zeros_like(page_pair))
    return (attn_out, decode_pages)


VMEM_LIMIT = 48 * 1024 * 1024
CHUNK = 512
SUM_ROWS = 16


def in_vmem(count):
    return [pl.BlockSpec(memory_space=pltpu.VMEM)] * count


def in_smem(count):
    return [pl.BlockSpec(memory_space=pltpu.SMEM)] * count


def params():
    return pltpu.CompilerParams(vmem_limit_bytes=VMEM_LIMIT)


def cost(flops, nbytes):
    return pl.CostEstimate(flops=flops, bytes_accessed=nbytes, transcendentals=0)


def nt_dot(left, right):
    return lax.dot_general(
        left, right, (((1,), (1,)), ((), ())), preferred_element_type=jnp.float32
    )


def holder_of(page, pool_dev):
    if pool_dev & (pool_dev - 1) == 0:
        return jnp.right_shift(page, pool_dev.bit_length() - 1)
    return page // pool_dev


def pick_pages_kernel(place_ref, hits_ref, pool_ref, mine_ref, other_ref, held, sems):
    me, head = place_ref[0], place_ref[1]
    pool_dev, page_len = pool_ref.shape[0], pool_ref.shape[1]
    slots = held.shape[0]
    rows = 2 * page_len
    out_row = lax.broadcasted_iota(jnp.int32, (rows, rows), 0)
    in_row = lax.broadcasted_iota(jnp.int32, (rows, rows), 1)
    wanted = jnp.where(out_row < page_len, 2 * out_row, 2 * (out_row - page_len) + 1)
    unweave = (in_row == wanted).astype(jnp.bfloat16)

    def fetch(page, slot):
        return pltpu.make_async_copy(pool_ref.at[page], held.at[slot], sems.at[slot])

    def entry(e, count):
        page = hits_ref[e]
        is_mine = (page >= 0) & (holder_of(page, pool_dev) == me)

        @pl.when(is_mine)
        def _():
            fetch(page - me * pool_dev, count).start()

        return count + is_mine.astype(jnp.int32)

    count = lax.fori_loop(0, hits_ref.shape[0], entry, jnp.int32(0))

    def arrive(slot, carry):
        fetch(0, slot).wait()
        return carry

    lax.fori_loop(0, count, arrive, 0)
    for slot in range(slots):
        at = slice(slot * rows, (slot + 1) * rows)
        slab = held[slot]
        first = slab[:, :, :128].reshape(rows, 128)
        second = slab[:, :, 128:].reshape(rows, 128)
        both = jnp.concatenate([first, second], axis=1)
        both = jnp.dot(unweave, both, preferred_element_type=jnp.float32)
        both = both.astype(jnp.bfloat16)
        mine_ref[at, :] = jnp.where(head == 0, both[:, :128], both[:, 128:])
        other_ref[at, :] = jnp.where(head == 0, both[:, 128:], both[:, :128])


def pick_pages(place, hits, pool, slots):
    rows = slots * 2 * pool.shape[1]
    block = jax.ShapeDtypeStruct((rows, 128), jnp.bfloat16)
    return pl.pallas_call(
        pick_pages_kernel,
        out_shape=(block, block),
        in_specs=in_smem(2) + [pl.BlockSpec(memory_space=pl.ANY)],
        out_specs=tuple(in_vmem(2)),
        scratch_shapes=[
            pltpu.VMEM((slots,) + pool.shape[1:], jnp.bfloat16),
            pltpu.SemaphoreType.DMA((slots,)),
        ],
        compiler_params=params(),
        cost_estimate=cost(0, 4 * pool.size),
        name="pick_pages",
    )(place, hits, pool)


def column_to_row(column):
    return jnp.transpose(jnp.broadcast_to(column, (128, 128)))[0:1]


def row_to_column(row):
    return jnp.transpose(jnp.broadcast_to(row, (128, 128)))[:, 0:1]


def plane_order(plane):
    return [0, jnp.where(plane <= 2, 1, 3), 2, jnp.where(plane <= 2, 3, 1)]


def pack_weights_kernel(place_ref, wq_ref, wk_ref, wv_ref, own_ref, core_ref, side_ref):
    plane, lane = place_ref[2], place_ref[3]
    feats = wk_ref.shape[0]
    block = wq_ref.shape[0] // 16
    half = own_ref.shape[0]
    for r, out_ref in enumerate((own_ref, core_ref, side_ref, side_ref)):
        base = half if r == 3 else 0
        for k, offset in enumerate(plane_order(plane)):
            start = (((plane + offset) & 3) * 4 + (lane ^ r)) * block
            start = pl.multiple_of(start, block)
            out_ref[base + k * block : base + (k + 1) * block, :] = wq_ref[pl.ds(start, block), :]
            for j in range(block // 128):
                at = base + 4 * block + (k * (block // 128) + j) * 2 * feats
                columns = pl.ds(pl.multiple_of(start + j * 128, 128), 128)
                out_ref[at : at + feats, :] = wk_ref[:, columns]
                out_ref[at + feats : at + 2 * feats, :] = wv_ref[:, columns]


def pack_weights(place, wq, wk_t, wv_t):
    rows = wq.shape[0] // 4 + 2 * wk_t.shape[0] * wk_t.shape[1] // 4 // 128
    block = jax.ShapeDtypeStruct((rows, 128), jnp.bfloat16)
    return pl.pallas_call(
        pack_weights_kernel,
        out_shape=(block, block, jax.ShapeDtypeStruct((2 * rows, 128), jnp.bfloat16)),
        in_specs=in_smem(1) + in_vmem(3),
        out_specs=tuple(in_vmem(3)),
        compiler_params=params(),
        cost_estimate=cost(1, 1),
        name="pack_weights",
    )(place, wq, wk_t, wv_t)


def project_block(k, raw, inv, gain_ref, weights, block):
    chunks = block // 128
    normed = (raw.astype(jnp.float32) * inv * gain_ref[k : k + 1, :]).astype(jnp.bfloat16)
    wide = jnp.concatenate([ref[k * block : (k + 1) * block, :] for ref in weights], axis=1)
    kv_rows = []
    for ref in weights:
        pieces = []
        for j in range(chunks):
            at = 4 * block + (k * chunks + j) * 32
            pieces.append(ref[at : at + 32, :])
        kv_rows.append(jnp.concatenate(pieces, axis=1))
    parts = jnp.dot(normed, wide, preferred_element_type=jnp.float32)
    return parts, nt_dot(jnp.concatenate(kv_rows, axis=0), normed)


def add_sums_kernel(hidden_ref, squares_ref, out_ref):
    toks = hidden_ref.shape[0]
    out_ref[:toks, :] = hidden_ref[...]
    left = squares_ref[...]
    rows = []
    for _ in range(3):
        rows.append(left.astype(jnp.bfloat16).astype(jnp.float32))
        left = left - rows[-1]
    rows.append(jnp.zeros((SUM_ROWS - 3, toks), jnp.float32))
    out_ref[toks:, :] = jnp.concatenate(rows, axis=0).astype(jnp.bfloat16)


def add_sums(hidden, squares):
    toks, block = hidden.shape
    return pl.pallas_call(
        add_sums_kernel,
        out_shape=jax.ShapeDtypeStruct((toks + SUM_ROWS, block), jnp.bfloat16),
        in_specs=in_vmem(2),
        out_specs=in_vmem(1)[0],
        compiler_params=params(),
        cost_estimate=cost(0, 1 << 20),
        name="add_sums",
    )(hidden, squares.reshape(1, toks))


def project_kernel(place_ref, gain_ref, own_ref, *refs):
    downs, ups, weights, out_refs = refs[0:3], refs[3:6], refs[6:10], refs[10:]
    plane = place_ref[2]
    block = own_ref.shape[1]
    toks = own_ref.shape[0] - SUM_ROWS
    sources = (
        lambda at: own_ref[at],
        lambda at: jnp.where(plane <= 2, downs[0][at], ups[0][at]),
        lambda at: jnp.where(plane <= 1, downs[1][at], ups[1][at]),
        lambda at: jnp.where(
            plane == 0, downs[2][at], jnp.where(plane == 3, ups[2][at], ups[0][at])
        ),
    )
    squares = sum(
        jnp.sum(source(slice(toks, toks + SUM_ROWS)).astype(jnp.float32), axis=0, keepdims=True)
        for source in sources
    )
    inv = lax.rsqrt(squares / (block * 16) + EPS)
    inv = jnp.concatenate(
        [row_to_column(inv[:, t : t + 128]) for t in range(0, toks, 128)], axis=0
    )
    query, kv_total = None, None
    for k, source in enumerate(sources):
        parts, kv_part = project_block(k, source(slice(0, toks)), inv, gain_ref, weights, block)
        query = parts if k == 0 else query + parts
        kv_total = kv_part if k == 0 else kv_total + kv_part
    half = toks // 2
    for n, out_ref in enumerate(out_refs):
        r, rows = n // 2, slice(n % 2 * half, (n % 2 + 1) * half)
        out_ref[:half, :] = query[rows, r * 128 : (r + 1) * 128]
        for t in range(half // 128):
            chunk = slice(rows.start + t * 128, rows.start + (t + 1) * 128)
            out_ref[half + t * 32 : half + (t + 1) * 32, :] = kv_total[r * 32 : (r + 1) * 32, chunk]


def project(place, gain, downs, ups, weights):
    toks = downs[0].shape[0] - SUM_ROWS
    out = jax.ShapeDtypeStruct(((toks + 128) // 2, 128), jnp.float32)
    return pl.pallas_call(
        project_kernel,
        out_shape=(out,) * 8,
        in_specs=in_smem(1) + in_vmem(12),
        out_specs=tuple(in_vmem(8)),
        compiler_params=params(),
        cost_estimate=cost(2 * toks * 512 * 640, 6 << 20),
        name="project",
    )(place, gain, *downs, *ups[1:], *weights)


def finish_kernel(*refs):
    cos_ref, sin_ref, out_ref = refs[6:]
    toks = cos_ref.shape[0]
    half, kv_rows = toks // 2, 64
    for n in range(2):
        rows = slice(n * half, (n + 1) * half)
        total = refs[n][...] + refs[2 + n][...] + refs[4 + n][...]
        query = total[:half]
        swapped = jnp.concatenate([query[:, 64:], query[:, :64]], axis=1)
        rotated = query * cos_ref[rows, :] + swapped * sin_ref[rows, :]
        out_ref[rows, :] = rotated.astype(jnp.bfloat16)
        at = toks + n * kv_rows
        out_ref[at : at + kv_rows, :] = total[half:].astype(jnp.bfloat16)


def finish(own, got, far_sum, cos_wide, sin_wide):
    toks = cos_wide.shape[0]
    return pl.pallas_call(
        finish_kernel,
        out_shape=jax.ShapeDtypeStruct((toks + 128, 128), jnp.bfloat16),
        in_specs=in_vmem(8),
        out_specs=in_vmem(1)[0],
        compiler_params=params(),
        cost_estimate=cost(0, 2 << 20),
        name="finish_projection",
    )(*own, *got, *far_sum, cos_wide, sin_wide)


def lane_tiles(values, join):
    joined = values[:, :128]
    for start in range(128, values.shape[1], 128):
        joined = join(joined, values[:, start : start + 128])
    return joined


def put_state(out_ref, toks, first, acc, top, total):
    out_ref[first : first + acc.shape[0], :] = acc
    for b in range(acc.shape[0] // 128):
        row, part = toks + first // 128 + b, slice(b * 128, (b + 1) * 128)
        out_ref[row : row + 1, :] = column_to_row(top[part])
        out_ref[row + 4 : row + 5, :] = column_to_row(total[part])


def get_state(ref, toks, first, count):
    rows = range(toks + first // 128, toks + (first + count) // 128)
    top = [row_to_column(ref[row : row + 1, :]) for row in rows]
    total = [row_to_column(ref[row + 4 : row + 5, :]) for row in rows]
    return ref[first : first + count, :], jnp.concatenate(top), jnp.concatenate(total)


def merge_states(states):
    peak = functools.reduce(jnp.maximum, [top for _, top, _ in states])
    base = jnp.where(peak == -jnp.inf, 0.0, peak)
    fades = [jnp.exp(top - base) for _, top, _ in states]
    acc = sum(acc * fade for (acc, _, _), fade in zip(states, fades))
    total = sum(total * fade for (_, _, total), fade in zip(states, fades))
    return acc, peak, total


def attend_kernel(offset, page_len, earlier, table_ref, *refs):
    blocks, (own_ref, far_ref), refs = refs[:4], refs[4:6], refs[6:]
    before = refs[:2] if earlier else ()
    outs, (held, keys, values, scores_ref, acc, lanes, sems) = refs[-9:-7], refs[-7:]
    copies = [
        pltpu.make_async_copy(block, held.at[n, pl.ds(0, block.shape[0])], sems.at[n])
        for n, block in enumerate(blocks)
    ]
    for copy in copies:
        copy.start()
    me = table_ref[0] ^ offset
    toks = outs[0].shape[0] - 8
    new_len = toks // 2
    chunk_pages = CHUNK // page_len
    for copy in copies:
        copy.wait()
    for request in range(2):
        last_holder = table_ref[1 + request]
        has_last = (last_holder & 12) == (me & 12)
        pages = jnp.int32(0)
        for n in range(4):
            holder = (me & 12) | ((last_holder + 1 + n) & 3)
            count = table_ref[5 + request * 16 + holder]
            first = table_ref[5 + holder] if request else jnp.int32(0)
            which = (holder ^ me) & 3

            def move(p, carry, which=which, first=first, pages=pages):
                source = pl.multiple_of((first + 4 * p) * 2 * page_len, 2 * page_len)
                target = pl.multiple_of((pages + 4 * p) * page_len, page_len)
                slab = held[which, pl.ds(source, 8 * page_len), :]
                slab = slab.reshape(4, 2 * page_len, 128)
                four = pl.ds(target, 4 * page_len)
                keys[four, :] = slab[:, :page_len].reshape(4 * page_len, 128)
                values[four, :] = slab[:, page_len:].reshape(4 * page_len, 128)
                return carry

            lax.fori_loop(0, (count + 3) // 4, move, 0)
            pages = pages + count
        trips = (pages + chunk_pages - 1) // chunk_pages

        rest = pl.ds(pl.multiple_of(pages * page_len, page_len), CHUNK)
        values[rest, :] = jnp.zeros((CHUNK, 128), jnp.bfloat16)
        keys_here = pages * page_len - jnp.where(has_last, table_ref[3 + request], 0)
        rows = slice(request * new_len, (request + 1) * new_len)
        query = jnp.concatenate([far_ref[rows, :], own_ref[rows, :]], axis=0)
        lanes[...] = jnp.full_like(lanes, -jnp.inf)

        def score(n, carry, query=query, keys_here=keys_here):
            at = pl.ds(pl.multiple_of(n * CHUNK, CHUNK), CHUNK)
            scores = nt_dot(query, keys[at, :]) * 128**-0.5
            column = lax.broadcasted_iota(jnp.int32, scores.shape, 1)
            scores = jnp.where(column < keys_here - n * CHUNK, scores, -jnp.inf)
            scores_ref[:, at] = scores
            lanes[...] = jnp.maximum(lanes[...], lane_tiles(scores, jnp.maximum))
            return carry

        lax.fori_loop(0, trips, score, 0)
        top = jnp.max(lanes[...], axis=1, keepdims=True)
        lanes[...] = jnp.zeros_like(lanes)
        acc[...] = jnp.zeros_like(acc)

        def mix(n, carry, top=top):
            at = pl.ds(pl.multiple_of(n * CHUNK, CHUNK), CHUNK)
            exps = jnp.exp(scores_ref[:, at] - top)
            lanes[...] += lane_tiles(exps, jnp.add)
            acc[...] += jnp.dot(
                exps.astype(jnp.bfloat16), values[at, :], preferred_element_type=jnp.float32
            )
            return carry

        lax.fori_loop(0, trips, mix, 0)
        total = jnp.sum(lanes[...], axis=1, keepdims=True)
        for n, out_ref in enumerate(outs):
            part = slice(n * new_len, (n + 1) * new_len)
            state = (acc[part, :], top[part], total[part])
            if earlier:
                past = get_state(before[n], toks, request * new_len, new_len)
                state = merge_states([past, state])
            put_state(out_ref, toks, request * new_len, *state)


def attend(offset, table, blocks, own_query, far_query, earlier, toks, span, page_len):
    new_len = toks // 2
    state = jax.ShapeDtypeStruct((toks + 8, 128), jnp.float32)
    return pl.pallas_call(
        functools.partial(attend_kernel, offset, page_len, bool(earlier)),
        out_shape=(state, state),
        in_specs=in_smem(1)
        + [pl.BlockSpec(memory_space=pl.ANY)] * 4
        + in_vmem(2 + len(earlier)),
        out_specs=tuple(in_vmem(2)),
        scratch_shapes=[
            pltpu.VMEM((4, blocks[0].shape[0] + 8 * page_len, 128), jnp.bfloat16),
            pltpu.VMEM((span + CHUNK, 128), jnp.bfloat16),
            pltpu.VMEM((span + CHUNK, 128), jnp.bfloat16),
            pltpu.VMEM((toks, span), jnp.float32),
            pltpu.VMEM((toks, 128), jnp.float32),
            pltpu.VMEM((toks, 128), jnp.float32),
            pltpu.SemaphoreType.DMA((4,)),
        ],
        compiler_params=params(),
        cost_estimate=cost(1, 20 << 20),
        name="attend_far_plane" if offset else "attend_own_plane",
    )(table, *blocks, own_query, far_query, *earlier)


def new_tokens_kernel(
    place_ref, near_ref, side_ref, core_ref, cos_ref, sin_ref, query_ref, state_ref, page_ref, held, kt, vt
):
    me, head = place_ref[0], place_ref[1]
    toks = cos_ref.shape[1]
    for n in range(4):
        held[n] = near_ref[n]
        held[4 + n] = side_ref[n]
    for n in range(8):
        held[8 + n] = core_ref[n]
    for device in range(16):
        rel = device ^ me
        block = held[(rel & 1) * 8 + ((rel >> 1) & 1) * 4 + (rel >> 2)]
        rows = slice((device % 8) * 16, (device % 8) * 16 + 16)
        for t in range(toks // 128):
            columns = slice(t * 128, (t + 1) * 128)
            kt[device // 8, rows, columns] = block[t * 32 : t * 32 + 16]
            vt[device // 8, rows, columns] = block[t * 32 + 16 : t * 32 + 32]
    cos, sin = cos_ref[...], sin_ref[...]
    for g in range(2):
        first = kt[g, :64, :].astype(jnp.float32)
        second = kt[g, 64:, :].astype(jnp.float32)
        kt[g, :64, :] = (first * cos - second * sin).astype(jnp.bfloat16)
        kt[g, 64:, :] = (second * cos + first * sin).astype(jnp.bfloat16)
    new_len = toks // 2
    query_at = lax.broadcasted_iota(jnp.int32, (new_len, new_len), 0)
    key_at = lax.broadcasted_iota(jnp.int32, (new_len, new_len), 1)
    for request in range(2):
        part = slice(request * new_len, (request + 1) * new_len)
        scores = jnp.dot(
            query_ref[part, :], kt[head, :, part], preferred_element_type=jnp.float32
        )
        scores = jnp.where(key_at <= query_at, scores * 128**-0.5, -jnp.inf)
        top = jnp.max(scores, axis=1, keepdims=True)
        exps = jnp.exp(scores - top)
        acc = nt_dot(exps.astype(jnp.bfloat16), vt[head, :, part])
        total = jnp.sum(exps, axis=1, keepdims=True)
        put_state(state_ref, toks, request * new_len, acc, top, total)
    page_len = page_ref.shape[1]
    out_row = lax.broadcasted_iota(jnp.int32, (2 * page_len, 128), 0)
    token = lax.broadcasted_iota(jnp.int32, (2 * page_len, 128), 1)
    for slot in range(page_ref.shape[0]):
        row, has = place_ref[4 + 2 * slot], place_ref[5 + 2 * slot]
        start = (row // 8) * (toks // 2) + ((row // 2) % 4) * page_len
        columns = pl.ds(pl.multiple_of(start // 128 * 128, 128), 128)
        inside = token - start % 128
        inside = jnp.where(has > 0, inside, -1)
        take_k = ((out_row % 2 == 0) & (inside == out_row // 2)).astype(jnp.bfloat16)
        take_v = ((out_row % 2 == 1) & (inside == out_row // 2)).astype(jnp.bfloat16)
        woven = nt_dot(take_k, kt[row % 2, :, columns]) + nt_dot(take_v, vt[row % 2, :, columns])
        page_ref[slot] = woven.astype(jnp.bfloat16).reshape(page_len, 2, 128)


def new_tokens(place, near, side, core, cos_t, sin_t, query_kv, page_len):
    toks = cos_t.shape[1]
    return pl.pallas_call(
        new_tokens_kernel,
        out_shape=(
            jax.ShapeDtypeStruct((toks + 8, 128), jnp.float32),
            jax.ShapeDtypeStruct((OWN, page_len, 2, 128), jnp.bfloat16),
        ),
        in_specs=in_smem(1) + in_vmem(6),
        out_specs=tuple(in_vmem(2)),
        scratch_shapes=[
            pltpu.VMEM((16, 128, 128), jnp.bfloat16),
            pltpu.VMEM((2, 128, toks), jnp.bfloat16),
            pltpu.VMEM((2, 128, toks), jnp.bfloat16),
        ],
        compiler_params=params(),
        cost_estimate=cost(0, 2 << 20),
        name="new_tokens",
    )(place, near, side, core, cos_t, sin_t, query_kv)


def combine_kernel(own_ref, far_ref, new_ref, out_ref):
    toks = out_ref.shape[0]
    for first in range(0, toks, 128):
        states = [get_state(ref, toks, first, 128) for ref in (own_ref, far_ref, new_ref)]
        acc, _, total = merge_states(states)
        out_ref[first : first + 128, :] = (acc / total).astype(jnp.bfloat16)


def combine(own, far, new):
    toks = own.shape[0] - 8
    return pl.pallas_call(
        combine_kernel,
        out_shape=jax.ShapeDtypeStruct((toks, 128), jnp.bfloat16),
        in_specs=in_vmem(3),
        out_specs=in_vmem(1)[0],
        compiler_params=params(),
        cost_estimate=cost(0, 1 << 20),
        name="combine",
    )(own, far, new)


def swap(values, bits):
    return lax.ppermute(values, "inst", [(i, i ^ bits) for i in range(16)])


def after(values, *others):
    return lax.optimization_barrier((values, others))[0]


def hop(values, step, step_count):
    pairs = []
    for i in range(16):
        plane = i // 4
        sends = plane >= step_count - 1 if step > 0 else plane <= 4 - step_count
        if sends and 0 <= plane + step <= 3:
            pairs.append((i, i + 4 * step))
    return lax.ppermute(values, "inst", pairs)


def on_16_devices(
    hidden, gain, w_query, w_key, w_value, cache_pool, prefix_len, hit_page, decode_owner
):
    me = lax.axis_index("inst")
    plane, lane = me // 4, me % 4
    toks, block = hidden.shape
    pool_dev, page_len = cache_pool.shape[0], cache_pool.shape[1]
    requests = prefix_len.shape[0]
    new_len = toks // requests
    slots = pool_dev // 2
    head = me // 8
    rows_new = decode_owner.shape[0]
    row_ids = jnp.arange(rows_new, dtype=jnp.int32)
    before_rows = (decode_owner[None, :] == decode_owner[:, None]) & (
        row_ids[None, :] < row_ids[:, None]
    )
    slot_num = jnp.sum(before_rows.astype(jnp.int32), axis=1)
    owned = (decode_owner[None, :] == me) & (
        slot_num[None, :] == jnp.arange(OWN, dtype=jnp.int32)[:, None]
    )
    pick_row = jnp.sum(jnp.where(owned, row_ids[None, :], 0), axis=1)
    has_row = jnp.any(owned, axis=1).astype(jnp.int32)
    place = jnp.stack([me, head, plane, lane]).astype(jnp.int32)
    page_place = jnp.concatenate([place, jnp.stack([pick_row, has_row], 1).reshape(-1)])
    hits = hit_page.reshape(-1)

    holders = jnp.where(hit_page >= 0, hit_page // pool_dev, -1)
    counts = jnp.sum(
        (holders[:, :, None] == jnp.arange(16, dtype=jnp.int32)).astype(jnp.int32), axis=1
    )
    last_page = (prefix_len - 1) // page_len
    is_last = jnp.arange(hit_page.shape[1], dtype=jnp.int32)[None, :] == last_page[:, None]
    last_holder = jnp.sum(jnp.where(is_last, holders, 0), axis=1)
    missing = (last_page + 1) * page_len - prefix_len
    table = jnp.concatenate([me[None], last_holder, missing, counts.reshape(-1)]).astype(jnp.int32)

    wide = hidden.astype(jnp.float32)
    squares = jnp.sum(wide * wide, axis=1)
    for bit in (1, 2):
        squares = squares + swap(squares, bit)

    w_own, w_core, w_side = pack_weights(place, w_query, w_key.T, w_value.T)
    w_side = swap(after(w_side, squares), 2)
    rows = w_own.shape[0]
    weights = [w_own, swap(w_core, 1), w_side, swap(w_side[rows:], 1)]

    mine, other = pick_pages(place, hits, cache_pool, slots)
    first = add_sums(hidden, squares)
    downs, ups = [first], [first]
    for k in (1, 2, 3):
        down, up = downs[-1], ups[-1]
        if k == 2:
            down, up = after((down, up), mine)
        downs.append(hop(down, -1, k))
        ups.append(hop(up, 1, k))

    mine_side = swap(after(mine, w_side), 2)
    far_pages = swap(after(other, downs[2], ups[2]), 8)

    positions = (
        jnp.repeat(prefix_len, new_len) + jnp.tile(jnp.arange(new_len, dtype=jnp.int32), requests)
    ).astype(jnp.float32)
    cos_table, sin_table = rotary_tables(positions, 128)
    cos_wide = jnp.concatenate([cos_table, cos_table], axis=1)
    sin_wide = jnp.concatenate([-sin_table, sin_table], axis=1)

    gain_blocks = lax.dynamic_index_in_dim(gain.reshape(4, 4, block), lane, 1, keepdims=False)
    gain_blocks = gain_blocks[(plane + jnp.stack(plane_order(plane))) & 3]
    sums = project(place, gain_blocks, downs, ups, weights)
    got = [swap(part, 1) for part in sums[2:4] + sums[6:8]]
    far_sum = [swap(sums[4 + n] + got[2 + n], 2) for n in range(2)]
    far_sum = after(far_sum, far_pages)
    query_kv = finish(sums[:2], got[:2], far_sum, cos_wide, sin_wide)

    far_pages = after(far_pages, far_sum)
    far_side = swap(far_pages, 2)
    near_pages = [mine, swap(mine, 1), mine_side, swap(mine_side, 1)]
    away_pages = [far_pages, swap(far_pages, 1), far_side, swap(far_side, 1)]

    from_plane = swap(query_kv, 4)
    kv = query_kv[toks:]
    pair_kv = jnp.stack([kv, from_plane[toks:]])
    far_kv = swap(pair_kv, 8)

    span = hit_page.shape[1] * page_len
    sizes = (toks, span, page_len)
    part = attend(0, table, near_pages, query_kv, from_plane, (), *sizes)
    far_kv = after(far_kv, part)
    near_kv = jnp.concatenate([pair_kv, far_kv], axis=0)
    side_kv = swap(near_kv, 2)
    core_kv = swap(jnp.concatenate([near_kv, side_kv], axis=0), 1)
    partner_part, own_part = attend(8, table, away_pages, query_kv, from_plane, part, *sizes)
    partner_part = swap(partner_part, 4)
    new_part, decode_pages = new_tokens(
        page_place, near_kv, side_kv, core_kv, cos_table.T, sin_table.T, query_kv, page_len
    )
    attn_out = combine(own_part, partner_part, new_part)
    return (attn_out, decode_pages)


def solution(mesh):
    return jax.shard_map(
        on_16_devices if mesh.shape["inst"] == 16 else on_device,
        mesh=mesh,
        in_specs=(
            P("groups", "inst"),
            P(),
            P(None, "inst"),
            P(None, "inst"),
            P(None, "inst"),
            P(("groups", "inst"), None, None, None),
            P("groups"),
            P("groups", None),
            P("groups"),
        ),
        out_specs=(P("groups", "inst"), P(("groups", "inst"), None, None, None)),
        check_vma=False,
    )
```

```python
import functools

import jax
import jax.numpy as jnp
from jax import lax
from jax.experimental import pallas as pl
from jax.experimental.pallas import tpu as pltpu
from jax.sharding import PartitionSpec as P

OWN = 2


EPS = 1e-05
ROPE_BASE = 500000.0


def rotary_tables(positions, head_dim):
    half_dim = head_dim // 2
    freqs = ROPE_BASE ** (-(jnp.arange(half_dim, dtype=jnp.float32) * 2.0 / head_dim))
    angles = positions[:, None] * freqs[None, :]
    return (jnp.cos(angles), jnp.sin(angles))


def rotate_rows(values, cos_table, sin_table):
    half_dim = values.shape[-1] // 2
    first_half = values[..., :half_dim]
    second_half = values[..., half_dim:]
    return jnp.concatenate(
        [
            first_half * cos_table - second_half * sin_table,
            second_half * cos_table + first_half * sin_table,
        ],
        axis=-1,
    )


def rotate_cols(values, cos_table, sin_table):
    half_dim = values.shape[-2] // 2
    first_half = values[..., :half_dim, :]
    second_half = values[..., half_dim:, :]
    return jnp.concatenate(
        [
            first_half * cos_table - second_half * sin_table,
            second_half * cos_table + first_half * sin_table,
        ],
        axis=-2,
    )


def contract_last(left, right):
    return lax.dot_general(
        left, right, (((1,), (1,)), ((), ())), preferred_element_type=jnp.float32
    )


def contract_first(weights, rows):
    return lax.dot_general(
        weights, rows, (((0,), (1,)), ((), ())), preferred_element_type=jnp.float32
    )


def on_device(
    hidden, gain, w_query, w_key, w_value, cache_pool, prefix_len, hit_page, decode_owner
):
    my_index = lax.axis_index("inst")
    devices = lax.axis_size("inst")
    tok_count = hidden.shape[0]
    head_dim = w_query.shape[1]
    requests = prefix_len.shape[0]
    new_len = tok_count // requests
    gathered = lax.all_gather(hidden, "inst", axis=1, tiled=True)
    wide_vals = gathered.astype(jnp.float32)
    inverse_rms = lax.rsqrt(jnp.mean(wide_vals * wide_vals, axis=-1, keepdims=True) + EPS)
    normed = (wide_vals * inverse_rms * gain).astype(jnp.bfloat16)
    query = jnp.dot(normed, w_query, preferred_element_type=jnp.float32)
    key_cols = contract_first(w_key, normed)
    value_cols = contract_first(w_value, normed)
    new_kv = jnp.stack([key_cols.astype(jnp.bfloat16), value_cols.astype(jnp.bfloat16)])
    all_kv = lax.all_gather(new_kv, "inst", axis=1, tiled=True)
    kv_dim = all_kv.shape[1]
    kv_heads = kv_dim // head_dim
    group_size = devices // kv_heads
    my_group = my_index // group_size
    positions = (
        jnp.repeat(prefix_len, new_len) + jnp.tile(jnp.arange(new_len, dtype=jnp.int32), requests)
    ).astype(jnp.float32)
    cos_table, sin_table = rotary_tables(positions, head_dim)
    q_rot = rotate_rows(query, cos_table, sin_table).astype(jnp.bfloat16)
    k_rot = rotate_cols(
        all_kv[0].astype(jnp.float32).reshape(kv_heads, head_dim, tok_count),
        cos_table.T,
        sin_table.T,
    ).astype(jnp.bfloat16)
    v_heads = all_kv[1].reshape(kv_heads, head_dim, tok_count)
    my_keys = lax.dynamic_index_in_dim(k_rot, my_group, 0, keepdims=False)
    my_values = lax.dynamic_index_in_dim(v_heads, my_group, 0, keepdims=False)
    pool_dev = cache_pool.shape[0]
    page_len = cache_pool.shape[1]
    hit_slots = pool_dev // 2
    flat_hits = hit_page.reshape(-1)
    entries = flat_hits.shape[0]
    is_valid = flat_hits >= 0
    holder = jnp.where(is_valid, flat_hits // pool_dev, -1)
    pool_slot = jnp.where(is_valid, flat_hits % pool_dev, 0)
    entry_ids = jnp.arange(entries, dtype=jnp.int32)
    earlier = (
        (holder[None, :] == holder[:, None])
        & (entry_ids[None, :] < entry_ids[:, None])
        & is_valid[None, :]
    )
    ranking = jnp.sum(earlier.astype(jnp.int32), axis=1)
    mine = is_valid & (holder == my_index)
    chosen = mine[None, :] & (ranking[None, :] == jnp.arange(hit_slots, dtype=jnp.int32)[:, None])
    pool_index = jnp.sum(jnp.where(chosen, pool_slot[None, :], 0), axis=1)
    present = jnp.any(chosen, axis=1)
    picked = cache_pool[pool_index]
    picked = jnp.where(present[:, None, None, None], picked, jnp.zeros_like(picked))
    inv_scale = head_dim ** (-0.5)
    per_head = picked.reshape(hit_slots, page_len, 2, kv_heads, head_dim).transpose(3, 0, 1, 2, 4)
    outgoing = jnp.repeat(per_head, group_size, axis=0)
    incoming = lax.all_to_all(outgoing, "inst", split_axis=0, concat_axis=0, tiled=True)
    stacked = incoming.reshape(devices * hit_slots, page_len, 2, head_dim)
    where_from = jnp.where(is_valid, holder * hit_slots + ranking, 0)
    prefix_rows = stacked[where_from]
    prefix_keys = prefix_rows[:, :, 0].reshape(requests, -1, head_dim)
    prefix_values = prefix_rows[:, :, 1].reshape(requests, -1, head_dim)
    prefix_span = prefix_keys.shape[1]
    causal_ok = (
        jnp.arange(new_len, dtype=jnp.int32)[None, :]
        <= jnp.arange(new_len, dtype=jnp.int32)[:, None]
    )
    pieces = []
    for request in range(requests):
        lower = request * new_len
        q_part = q_rot[lower : lower + new_len]
        pre_scores = contract_last(q_part, prefix_keys[request]) * inv_scale
        new_scores = (
            jnp.dot(q_part, my_keys[:, lower : lower + new_len], preferred_element_type=jnp.float32)
            * inv_scale
        )
        prefix_ok = jnp.arange(prefix_span, dtype=jnp.int32)[None, :] < prefix_len[request]
        row_max = jnp.maximum(
            jnp.max(jnp.where(prefix_ok, pre_scores, -jnp.inf), axis=1),
            jnp.max(jnp.where(causal_ok, new_scores, -jnp.inf), axis=1),
        )[:, None]
        pre_exps = jnp.where(prefix_ok, jnp.exp(pre_scores - row_max), 0.0)
        new_exps = jnp.where(causal_ok, jnp.exp(new_scores - row_max), 0.0)
        row_sum = jnp.sum(pre_exps, axis=1, keepdims=True) + jnp.sum(
            new_exps, axis=1, keepdims=True
        )
        mixture = jnp.dot(
            pre_exps.astype(jnp.bfloat16),
            prefix_values[request],
            preferred_element_type=jnp.float32,
        )
        mixture = mixture + contract_last(
            new_exps.astype(jnp.bfloat16), my_values[:, lower : lower + new_len]
        )
        pieces.append((mixture / row_sum).astype(jnp.bfloat16))
    attn_out = jnp.concatenate(pieces, axis=0)
    pages_new = new_len // page_len
    rows_new = decode_owner.shape[0]
    k_pages = (
        k_rot.reshape(kv_heads, head_dim, requests, pages_new, page_len)
        .transpose(2, 3, 0, 4, 1)
        .reshape(rows_new, page_len, head_dim)
    )
    v_pages = (
        v_heads.reshape(kv_heads, head_dim, requests, pages_new, page_len)
        .transpose(2, 3, 0, 4, 1)
        .reshape(rows_new, page_len, head_dim)
    )
    row_ids = jnp.arange(rows_new, dtype=jnp.int32)
    before_rows = (decode_owner[None, :] == decode_owner[:, None]) & (
        row_ids[None, :] < row_ids[:, None]
    )
    slot_num = jnp.sum(before_rows.astype(jnp.int32), axis=1)
    owned = (decode_owner[None, :] == my_index) & (
        slot_num[None, :] == jnp.arange(OWN, dtype=jnp.int32)[:, None]
    )
    pick_row = jnp.sum(jnp.where(owned, row_ids[None, :], 0), axis=1)
    has_row = jnp.any(owned, axis=1)
    page_pair = jnp.stack([k_pages[pick_row], v_pages[pick_row]], axis=2)
    decode_pages = jnp.where(has_row[:, None, None, None], page_pair, jnp.zeros_like(page_pair))
    return (attn_out, decode_pages)


VMEM_LIMIT = 48 * 1024 * 1024
CHUNK = 1024
SUM_ROWS = 16


def in_vmem(count):
    return [pl.BlockSpec(memory_space=pltpu.VMEM)] * count


def in_smem(count):
    return [pl.BlockSpec(memory_space=pltpu.SMEM)] * count


def params():
    return pltpu.CompilerParams(vmem_limit_bytes=VMEM_LIMIT)


def cost(flops, nbytes):
    return pl.CostEstimate(flops=flops, bytes_accessed=nbytes, transcendentals=0)


def nt_dot(left, right):
    return lax.dot_general(
        left, right, (((1,), (1,)), ((), ())), preferred_element_type=jnp.float32
    )


def holder_of(page, pool_dev):
    if pool_dev & (pool_dev - 1) == 0:
        return jnp.right_shift(page, pool_dev.bit_length() - 1)
    return page // pool_dev


def pick_pages_kernel(place_ref, hits_ref, pool_ref, mine_ref, other_ref, held, sems):
    me, head = place_ref[0], place_ref[1]
    pool_dev, page_len = pool_ref.shape[0], pool_ref.shape[1]
    slots = held.shape[0]
    rows = 2 * page_len
    out_row = lax.broadcasted_iota(jnp.int32, (rows, rows), 0)
    in_row = lax.broadcasted_iota(jnp.int32, (rows, rows), 1)
    wanted = jnp.where(out_row < page_len, 2 * out_row, 2 * (out_row - page_len) + 1)
    unweave = (in_row == wanted).astype(jnp.bfloat16)

    def fetch(page, slot):
        return pltpu.make_async_copy(pool_ref.at[page], held.at[slot], sems.at[slot])

    def entry(e, count):
        page = hits_ref[e]
        is_mine = (page >= 0) & (holder_of(page, pool_dev) == me)

        @pl.when(is_mine)
        def _():
            fetch(page - me * pool_dev, count).start()

        return count + is_mine.astype(jnp.int32)

    count = lax.fori_loop(0, hits_ref.shape[0], entry, jnp.int32(0))

    def arrive(slot, carry):
        fetch(0, slot).wait()
        return carry

    lax.fori_loop(0, count, arrive, 0)
    for slot in range(slots):
        at = slice(slot * rows, (slot + 1) * rows)
        slab = held[slot]
        first = slab[:, :, :128].reshape(rows, 128)
        second = slab[:, :, 128:].reshape(rows, 128)
        both = jnp.concatenate([first, second], axis=1)
        both = jnp.dot(unweave, both, preferred_element_type=jnp.float32)
        both = both.astype(jnp.bfloat16)
        mine_ref[at, :] = jnp.where(head == 0, both[:, :128], both[:, 128:])
        other_ref[at, :] = jnp.where(head == 0, both[:, 128:], both[:, :128])


def pick_pages(place, hits, pool, slots):
    rows = slots * 2 * pool.shape[1]
    block = jax.ShapeDtypeStruct((rows, 128), jnp.bfloat16)
    return pl.pallas_call(
        pick_pages_kernel,
        out_shape=(block, block),
        in_specs=in_smem(2) + [pl.BlockSpec(memory_space=pl.ANY)],
        out_specs=tuple(in_vmem(2)),
        scratch_shapes=[
            pltpu.VMEM((slots,) + pool.shape[1:], jnp.bfloat16),
            pltpu.SemaphoreType.DMA((slots,)),
        ],
        compiler_params=params(),
        cost_estimate=cost(0, 4 * pool.size),
        name="pick_pages",
    )(place, hits, pool)


def column_to_row(column):
    return jnp.transpose(jnp.broadcast_to(column, (128, 128)))[0:1]


def row_to_column(row):
    return jnp.transpose(jnp.broadcast_to(row, (128, 128)))[:, 0:1]


def plane_order(plane):
    return [0, jnp.where(plane <= 2, 1, 3), 2, jnp.where(plane <= 2, 3, 1)]


def pack_weights_kernel(place_ref, wq_ref, wk_ref, wv_ref, own_ref, core_ref, side_ref):
    plane, lane = place_ref[2], place_ref[3]
    feats = wk_ref.shape[0]
    block = wq_ref.shape[0] // 16
    half = own_ref.shape[0]
    for r, out_ref in enumerate((own_ref, core_ref, side_ref, side_ref)):
        base = half if r == 3 else 0
        for k, offset in enumerate(plane_order(plane)):
            start = (((plane + offset) & 3) * 4 + (lane ^ r)) * block
            start = pl.multiple_of(start, block)
            out_ref[base + k * block : base + (k + 1) * block, :] = wq_ref[pl.ds(start, block), :]
            for j in range(block // 128):
                at = base + 4 * block + (k * (block // 128) + j) * 2 * feats
                columns = pl.ds(pl.multiple_of(start + j * 128, 128), 128)
                out_ref[at : at + feats, :] = wk_ref[:, columns]
                out_ref[at + feats : at + 2 * feats, :] = wv_ref[:, columns]


def pack_weights(place, wq, wk_t, wv_t):
    rows = wq.shape[0] // 4 + 2 * wk_t.shape[0] * wk_t.shape[1] // 4 // 128
    block = jax.ShapeDtypeStruct((rows, 128), jnp.bfloat16)
    return pl.pallas_call(
        pack_weights_kernel,
        out_shape=(block, block, jax.ShapeDtypeStruct((2 * rows, 128), jnp.bfloat16)),
        in_specs=in_smem(1) + in_vmem(3),
        out_specs=tuple(in_vmem(3)),
        compiler_params=params(),
        cost_estimate=cost(1, 1),
        name="pack_weights",
    )(place, wq, wk_t, wv_t)


def project_block(k, raw, inv, gain_ref, weights, block):
    chunks = block // 128
    normed = (raw.astype(jnp.float32) * inv * gain_ref[k : k + 1, :]).astype(jnp.bfloat16)
    wide = jnp.concatenate([ref[k * block : (k + 1) * block, :] for ref in weights], axis=1)
    kv_rows = []
    for ref in weights:
        pieces = []
        for j in range(chunks):
            at = 4 * block + (k * chunks + j) * 32
            pieces.append(ref[at : at + 32, :])
        kv_rows.append(jnp.concatenate(pieces, axis=1))
    parts = jnp.dot(normed, wide, preferred_element_type=jnp.float32)
    return parts, nt_dot(jnp.concatenate(kv_rows, axis=0), normed)


def add_sums_kernel(hidden_ref, squares_ref, out_ref):
    toks = hidden_ref.shape[0]
    out_ref[:toks, :] = hidden_ref[...]
    left = squares_ref[...]
    rows = []
    for _ in range(3):
        rows.append(left.astype(jnp.bfloat16).astype(jnp.float32))
        left = left - rows[-1]
    rows.append(jnp.zeros((SUM_ROWS - 3, toks), jnp.float32))
    out_ref[toks:, :] = jnp.concatenate(rows, axis=0).astype(jnp.bfloat16)


def add_sums(hidden, squares):
    toks, block = hidden.shape
    return pl.pallas_call(
        add_sums_kernel,
        out_shape=jax.ShapeDtypeStruct((toks + SUM_ROWS, block), jnp.bfloat16),
        in_specs=in_vmem(2),
        out_specs=in_vmem(1)[0],
        compiler_params=params(),
        cost_estimate=cost(0, 1 << 20),
        name="add_sums",
    )(hidden, squares.reshape(1, toks))


def project_kernel(place_ref, gain_ref, own_ref, *refs):
    downs, ups, weights, out_refs = refs[0:3], refs[3:6], refs[6:10], refs[10:]
    plane = place_ref[2]
    block = own_ref.shape[1]
    toks = own_ref.shape[0] - SUM_ROWS
    sources = (
        lambda at: own_ref[at],
        lambda at: jnp.where(plane <= 2, downs[0][at], ups[0][at]),
        lambda at: jnp.where(plane <= 1, downs[1][at], ups[1][at]),
        lambda at: jnp.where(
            plane == 0, downs[2][at], jnp.where(plane == 3, ups[2][at], ups[0][at])
        ),
    )
    squares = sum(
        jnp.sum(source(slice(toks, toks + SUM_ROWS)).astype(jnp.float32), axis=0, keepdims=True)
        for source in sources
    )
    inv = lax.rsqrt(squares / (block * 16) + EPS)
    inv = jnp.concatenate(
        [row_to_column(inv[:, t : t + 128]) for t in range(0, toks, 128)], axis=0
    )
    query, kv_total = None, None
    for k, source in enumerate(sources):
        parts, kv_part = project_block(k, source(slice(0, toks)), inv, gain_ref, weights, block)
        query = parts if k == 0 else query + parts
        kv_total = kv_part if k == 0 else kv_total + kv_part
    half = toks // 2
    for n, out_ref in enumerate(out_refs):
        r, rows = n // 2, slice(n % 2 * half, (n % 2 + 1) * half)
        out_ref[:half, :] = query[rows, r * 128 : (r + 1) * 128]
        for t in range(half // 128):
            chunk = slice(rows.start + t * 128, rows.start + (t + 1) * 128)
            out_ref[half + t * 32 : half + (t + 1) * 32, :] = kv_total[r * 32 : (r + 1) * 32, chunk]


def project(place, gain, downs, ups, weights):
    toks = downs[0].shape[0] - SUM_ROWS
    out = jax.ShapeDtypeStruct(((toks + 128) // 2, 128), jnp.float32)
    return pl.pallas_call(
        project_kernel,
        out_shape=(out,) * 8,
        in_specs=in_smem(1) + in_vmem(12),
        out_specs=tuple(in_vmem(8)),
        compiler_params=params(),
        cost_estimate=cost(2 * toks * 512 * 640, 6 << 20),
        name="project",
    )(place, gain, *downs, *ups[1:], *weights)


def finish_kernel(*refs):
    cos_ref, sin_ref, out_ref = refs[6:]
    toks = cos_ref.shape[0]
    half, kv_rows = toks // 2, 64
    for n in range(2):
        rows = slice(n * half, (n + 1) * half)
        total = refs[n][...] + refs[2 + n][...] + refs[4 + n][...]
        query = total[:half]
        swapped = jnp.concatenate([query[:, 64:], query[:, :64]], axis=1)
        rotated = query * cos_ref[rows, :] + swapped * sin_ref[rows, :]
        out_ref[rows, :] = rotated.astype(jnp.bfloat16)
        at = toks + n * kv_rows
        out_ref[at : at + kv_rows, :] = total[half:].astype(jnp.bfloat16)


def finish(own, got, far_sum, cos_wide, sin_wide):
    toks = cos_wide.shape[0]
    return pl.pallas_call(
        finish_kernel,
        out_shape=jax.ShapeDtypeStruct((toks + 128, 128), jnp.bfloat16),
        in_specs=in_vmem(8),
        out_specs=in_vmem(1)[0],
        compiler_params=params(),
        cost_estimate=cost(0, 2 << 20),
        name="finish_projection",
    )(*own, *got, *far_sum, cos_wide, sin_wide)


def lane_tiles(values, join):
    joined = values[:, :128]
    for start in range(128, values.shape[1], 128):
        joined = join(joined, values[:, start : start + 128])
    return joined


def put_state(out_ref, toks, first, acc, top, total):
    out_ref[first : first + acc.shape[0], :] = acc
    for b in range(acc.shape[0] // 128):
        row, part = toks + first // 128 + b, slice(b * 128, (b + 1) * 128)
        out_ref[row : row + 1, :] = column_to_row(top[part])
        out_ref[row + 4 : row + 5, :] = column_to_row(total[part])


def get_state(ref, toks, first, count):
    rows = range(toks + first // 128, toks + (first + count) // 128)
    top = [row_to_column(ref[row : row + 1, :]) for row in rows]
    total = [row_to_column(ref[row + 4 : row + 5, :]) for row in rows]
    return ref[first : first + count, :], jnp.concatenate(top), jnp.concatenate(total)


def merge_states(states):
    peak = functools.reduce(jnp.maximum, [top for _, top, _ in states])
    base = jnp.where(peak == -jnp.inf, 0.0, peak)
    fades = [jnp.exp(top - base) for _, top, _ in states]
    acc = sum(acc * fade for (acc, _, _), fade in zip(states, fades))
    total = sum(total * fade for (_, _, total), fade in zip(states, fades))
    return acc, peak, total


def attend_kernel(offset, page_len, earlier, table_ref, *refs):
    blocks, (own_ref, far_ref), refs = refs[:4], refs[4:6], refs[6:]
    before = refs[:2] if earlier else ()
    outs, (held, keys, values, scores_ref, acc, lanes, sems) = refs[-9:-7], refs[-7:]
    copies = [
        pltpu.make_async_copy(block, held.at[n, pl.ds(0, block.shape[0])], sems.at[n])
        for n, block in enumerate(blocks)
    ]
    for copy in copies:
        copy.start()
    me = table_ref[0] ^ offset
    toks = outs[0].shape[0] - 8
    new_len = toks // 2
    chunk_pages = CHUNK // page_len
    for copy in copies:
        copy.wait()
    for request in range(2):
        last_holder = table_ref[1 + request]
        has_last = (last_holder & 12) == (me & 12)
        pages = jnp.int32(0)
        for n in range(4):
            holder = (me & 12) | ((last_holder + 1 + n) & 3)
            count = table_ref[5 + request * 16 + holder]
            first = table_ref[5 + holder] if request else jnp.int32(0)
            which = (holder ^ me) & 3

            def move(p, carry, which=which, first=first, pages=pages):
                source = pl.multiple_of((first + 4 * p) * 2 * page_len, 2 * page_len)
                target = pl.multiple_of((pages + 4 * p) * page_len, page_len)
                slab = held[which, pl.ds(source, 8 * page_len), :]
                slab = slab.reshape(4, 2 * page_len, 128)
                four = pl.ds(target, 4 * page_len)
                keys[four, :] = slab[:, :page_len].reshape(4 * page_len, 128)
                values[four, :] = slab[:, page_len:].reshape(4 * page_len, 128)
                return carry

            lax.fori_loop(0, (count + 3) // 4, move, 0)
            pages = pages + count
        trips = (pages + chunk_pages - 1) // chunk_pages

        rest = pl.ds(pl.multiple_of(pages * page_len, page_len), CHUNK)
        values[rest, :] = jnp.zeros((CHUNK, 128), jnp.bfloat16)
        keys_here = pages * page_len - jnp.where(has_last, table_ref[3 + request], 0)
        rows = slice(request * new_len, (request + 1) * new_len)
        query = jnp.concatenate([far_ref[rows, :], own_ref[rows, :]], axis=0)
        lanes[...] = jnp.full_like(lanes, -jnp.inf)

        def score(n, carry, query=query, keys_here=keys_here):
            at = pl.ds(pl.multiple_of(n * CHUNK, CHUNK), CHUNK)
            scores = nt_dot(query, keys[at, :]) * 128**-0.5
            column = lax.broadcasted_iota(jnp.int32, scores.shape, 1)
            scores = jnp.where(column < keys_here - n * CHUNK, scores, -jnp.inf)
            scores_ref[:, at] = scores
            lanes[...] = jnp.maximum(lanes[...], lane_tiles(scores, jnp.maximum))
            return carry

        lax.fori_loop(0, trips, score, 0)
        top = jnp.max(lanes[...], axis=1, keepdims=True)
        lanes[...] = jnp.zeros_like(lanes)
        acc[...] = jnp.zeros_like(acc)

        def mix(n, carry, top=top):
            at = pl.ds(pl.multiple_of(n * CHUNK, CHUNK), CHUNK)
            exps = jnp.exp(scores_ref[:, at] - top)
            lanes[...] += lane_tiles(exps, jnp.add)
            acc[...] += jnp.dot(
                exps.astype(jnp.bfloat16), values[at, :], preferred_element_type=jnp.float32
            )
            return carry

        lax.fori_loop(0, trips, mix, 0)
        total = jnp.sum(lanes[...], axis=1, keepdims=True)
        for n, out_ref in enumerate(outs):
            part = slice(n * new_len, (n + 1) * new_len)
            state = (acc[part, :], top[part], total[part])
            if earlier:
                past = get_state(before[n], toks, request * new_len, new_len)
                state = merge_states([past, state])
            put_state(out_ref, toks, request * new_len, *state)


def attend(offset, table, blocks, own_query, far_query, earlier, toks, span, page_len):
    new_len = toks // 2
    state = jax.ShapeDtypeStruct((toks + 8, 128), jnp.float32)
    return pl.pallas_call(
        functools.partial(attend_kernel, offset, page_len, bool(earlier)),
        out_shape=(state, state),
        in_specs=in_smem(1)
        + [pl.BlockSpec(memory_space=pl.ANY)] * 4
        + in_vmem(2 + len(earlier)),
        out_specs=tuple(in_vmem(2)),
        scratch_shapes=[
            pltpu.VMEM((4, blocks[0].shape[0] + 8 * page_len, 128), jnp.bfloat16),
            pltpu.VMEM((span + CHUNK, 128), jnp.bfloat16),
            pltpu.VMEM((span + CHUNK, 128), jnp.bfloat16),
            pltpu.VMEM((toks, span), jnp.float32),
            pltpu.VMEM((toks, 128), jnp.float32),
            pltpu.VMEM((toks, 128), jnp.float32),
            pltpu.SemaphoreType.DMA((4,)),
        ],
        compiler_params=params(),
        cost_estimate=cost(1, 20 << 20),
        name="attend_far_plane" if offset else "attend_own_plane",
    )(table, *blocks, own_query, far_query, *earlier)


def new_tokens_kernel(
    place_ref, near_ref, side_ref, core_ref, across_ref, cos_ref, sin_ref, query_ref, state_ref, page_ref, held, kt, vt
):
    me, head = place_ref[0], place_ref[1]
    toks = cos_ref.shape[1]
    for n in range(4):
        held[n] = near_ref[n]
        held[4 + n] = side_ref[n]
        held[8 + n] = core_ref[n]
        held[12 + n] = across_ref[n]
    for device in range(16):
        rel = device ^ me
        block = held[(rel & 1) * 8 + ((rel >> 1) & 1) * 4 + (rel >> 2)]
        rows = slice((device % 8) * 16, (device % 8) * 16 + 16)
        for t in range(toks // 128):
            columns = slice(t * 128, (t + 1) * 128)
            kt[device // 8, rows, columns] = block[t * 32 : t * 32 + 16]
            vt[device // 8, rows, columns] = block[t * 32 + 16 : t * 32 + 32]
    cos, sin = cos_ref[...], sin_ref[...]
    for g in range(2):
        first = kt[g, :64, :].astype(jnp.float32)
        second = kt[g, 64:, :].astype(jnp.float32)
        kt[g, :64, :] = (first * cos - second * sin).astype(jnp.bfloat16)
        kt[g, 64:, :] = (second * cos + first * sin).astype(jnp.bfloat16)
    new_len = toks // 2
    query_at = lax.broadcasted_iota(jnp.int32, (new_len, new_len), 0)
    key_at = lax.broadcasted_iota(jnp.int32, (new_len, new_len), 1)
    for request in range(2):
        part = slice(request * new_len, (request + 1) * new_len)
        scores = jnp.dot(
            query_ref[part, :], kt[head, :, part], preferred_element_type=jnp.float32
        )
        scores = jnp.where(key_at <= query_at, scores * 128**-0.5, -jnp.inf)
        top = jnp.max(scores, axis=1, keepdims=True)
        exps = jnp.exp(scores - top)
        acc = nt_dot(exps.astype(jnp.bfloat16), vt[head, :, part])
        total = jnp.sum(exps, axis=1, keepdims=True)
        put_state(state_ref, toks, request * new_len, acc, top, total)
    page_len = page_ref.shape[1]
    out_row = lax.broadcasted_iota(jnp.int32, (2 * page_len, 128), 0)
    token = lax.broadcasted_iota(jnp.int32, (2 * page_len, 128), 1)
    for slot in range(page_ref.shape[0]):
        row, has = place_ref[4 + 2 * slot], place_ref[5 + 2 * slot]
        start = (row // 8) * (toks // 2) + ((row // 2) % 4) * page_len
        columns = pl.ds(pl.multiple_of(start // 128 * 128, 128), 128)
        inside = token - start % 128
        inside = jnp.where(has > 0, inside, -1)
        take_k = ((out_row % 2 == 0) & (inside == out_row // 2)).astype(jnp.bfloat16)
        take_v = ((out_row % 2 == 1) & (inside == out_row // 2)).astype(jnp.bfloat16)
        woven = nt_dot(take_k, kt[row % 2, :, columns]) + nt_dot(take_v, vt[row % 2, :, columns])
        page_ref[slot] = woven.astype(jnp.bfloat16).reshape(page_len, 2, 128)


def new_tokens(place, near, side, core, across, cos_t, sin_t, query_kv, page_len):
    toks = cos_t.shape[1]
    return pl.pallas_call(
        new_tokens_kernel,
        out_shape=(
            jax.ShapeDtypeStruct((toks + 8, 128), jnp.float32),
            jax.ShapeDtypeStruct((OWN, page_len, 2, 128), jnp.bfloat16),
        ),
        in_specs=in_smem(1) + in_vmem(7),
        out_specs=tuple(in_vmem(2)),
        scratch_shapes=[
            pltpu.VMEM((16, 128, 128), jnp.bfloat16),
            pltpu.VMEM((2, 128, toks), jnp.bfloat16),
            pltpu.VMEM((2, 128, toks), jnp.bfloat16),
        ],
        compiler_params=params(),
        cost_estimate=cost(0, 2 << 20),
        name="new_tokens",
    )(place, near, side, core, across, cos_t, sin_t, query_kv)


def combine_kernel(own_ref, far_ref, new_ref, out_ref):
    toks = out_ref.shape[0]
    for first in range(0, toks, 128):
        states = [get_state(ref, toks, first, 128) for ref in (own_ref, far_ref, new_ref)]
        acc, _, total = merge_states(states)
        out_ref[first : first + 128, :] = (acc / total).astype(jnp.bfloat16)


def combine(own, far, new):
    toks = own.shape[0] - 8
    return pl.pallas_call(
        combine_kernel,
        out_shape=jax.ShapeDtypeStruct((toks, 128), jnp.bfloat16),
        in_specs=in_vmem(3),
        out_specs=in_vmem(1)[0],
        compiler_params=params(),
        cost_estimate=cost(0, 1 << 20),
        name="combine",
    )(own, far, new)


def swap(values, bits):
    return lax.ppermute(values, "inst", [(i, i ^ bits) for i in range(16)])


def after(values, *others):
    return lax.optimization_barrier((values, others))[0]


def hop(values, step, step_count):
    pairs = []
    for i in range(16):
        plane = i // 4
        sends = plane >= step_count - 1 if step > 0 else plane <= 4 - step_count
        if sends and 0 <= plane + step <= 3:
            pairs.append((i, i + 4 * step))
    return lax.ppermute(values, "inst", pairs)


def on_16_devices(
    hidden, gain, w_query, w_key, w_value, cache_pool, prefix_len, hit_page, decode_owner
):
    me = lax.axis_index("inst")
    plane, lane = me // 4, me % 4
    toks, block = hidden.shape
    pool_dev, page_len = cache_pool.shape[0], cache_pool.shape[1]
    requests = prefix_len.shape[0]
    new_len = toks // requests
    slots = pool_dev // 2
    head = me // 8
    rows_new = decode_owner.shape[0]
    row_ids = jnp.arange(rows_new, dtype=jnp.int32)
    before_rows = (decode_owner[None, :] == decode_owner[:, None]) & (
        row_ids[None, :] < row_ids[:, None]
    )
    slot_num = jnp.sum(before_rows.astype(jnp.int32), axis=1)
    owned = (decode_owner[None, :] == me) & (
        slot_num[None, :] == jnp.arange(OWN, dtype=jnp.int32)[:, None]
    )
    pick_row = jnp.sum(jnp.where(owned, row_ids[None, :], 0), axis=1)
    has_row = jnp.any(owned, axis=1).astype(jnp.int32)
    place = jnp.stack([me, head, plane, lane]).astype(jnp.int32)
    page_place = jnp.concatenate([place, jnp.stack([pick_row, has_row], 1).reshape(-1)])
    hits = hit_page.reshape(-1)

    holders = jnp.where(hit_page >= 0, hit_page // pool_dev, -1)
    counts = jnp.sum(
        (holders[:, :, None] == jnp.arange(16, dtype=jnp.int32)).astype(jnp.int32), axis=1
    )
    last_page = (prefix_len - 1) // page_len
    is_last = jnp.arange(hit_page.shape[1], dtype=jnp.int32)[None, :] == last_page[:, None]
    last_holder = jnp.sum(jnp.where(is_last, holders, 0), axis=1)
    missing = (last_page + 1) * page_len - prefix_len
    table = jnp.concatenate([me[None], last_holder, missing, counts.reshape(-1)]).astype(jnp.int32)

    wide = hidden.astype(jnp.float32)
    squares = jnp.sum(wide * wide, axis=1)
    for bit in (1, 2):
        squares = squares + swap(squares, bit)

    w_own, w_core, w_side = pack_weights(place, w_query, w_key.T, w_value.T)
    w_side = swap(after(w_side, squares), 2)
    rows = w_own.shape[0]
    weights = [w_own, swap(w_core, 1), w_side, swap(w_side[rows:], 1)]

    mine, other = pick_pages(place, hits, cache_pool, slots)
    first = add_sums(hidden, squares)
    downs, ups = [first], [first]
    for k in (1, 2, 3):
        down, up = downs[-1], ups[-1]
        if k == 2:
            down, up = after((down, up), mine)
        downs.append(hop(down, -1, k))
        ups.append(hop(up, 1, k))

    mine_side = swap(after(mine, w_side), 2)
    far_pages = swap(after(other, downs[2], ups[2]), 8)

    positions = (
        jnp.repeat(prefix_len, new_len) + jnp.tile(jnp.arange(new_len, dtype=jnp.int32), requests)
    ).astype(jnp.float32)
    cos_table, sin_table = rotary_tables(positions, 128)
    cos_wide = jnp.concatenate([cos_table, cos_table], axis=1)
    sin_wide = jnp.concatenate([-sin_table, sin_table], axis=1)

    gain_blocks = lax.dynamic_index_in_dim(gain.reshape(4, 4, block), lane, 1, keepdims=False)
    gain_blocks = gain_blocks[(plane + jnp.stack(plane_order(plane))) & 3]
    sums = project(place, gain_blocks, downs, ups, weights)
    got = [swap(part, 1) for part in sums[2:4] + sums[6:8]]
    got = after(got, mine_side)
    far_sum = [swap(sums[4 + n] + got[2 + n], 2) for n in range(2)]
    far_sum = after(far_sum, far_pages)
    query_kv = finish(sums[:2], got[:2], far_sum, cos_wide, sin_wide)

    far_pages = after(far_pages, far_sum)
    far_side = swap(far_pages, 2)
    near_pages = [mine, swap(mine, 1), mine_side, swap(mine_side, 1)]

    from_plane = swap(query_kv, 4)
    kv = query_kv[toks:]
    pair_kv = jnp.stack([kv, from_plane[toks:]])
    far_kv = swap(pair_kv, 8)

    span = hit_page.shape[1] * page_len
    sizes = (toks, span, page_len)
    part = attend(0, table, near_pages, query_kv, from_plane, (), *sizes)
    near_kv = jnp.concatenate([pair_kv, far_kv], axis=0)
    side_kv = swap(near_kv, 2)
    core_kv, across_kv = swap(near_kv, 1), swap(near_kv, 3)
    away_pages = [far_pages, swap(far_pages, 1), far_side, swap(after(far_side, part), 1)]
    partner_part, own_part = attend(8, table, away_pages, query_kv, from_plane, part, *sizes)
    partner_part = swap(partner_part, 4)
    new_part, decode_pages = new_tokens(
        page_place, near_kv, side_kv, core_kv, across_kv, cos_table.T, sin_table.T, query_kv, page_len
    )
    attn_out = combine(own_part, partner_part, new_part)
    return (attn_out, decode_pages)


def solution(mesh):
    return jax.shard_map(
        on_16_devices if mesh.shape["inst"] == 16 else on_device,
        mesh=mesh,
        in_specs=(
            P("groups", "inst"),
            P(),
            P(None, "inst"),
            P(None, "inst"),
            P(None, "inst"),
            P(("groups", "inst"), None, None, None),
            P("groups"),
            P("groups", None),
            P("groups"),
        ),
        out_specs=(P("groups", "inst"), P(("groups", "inst"), None, None, None)),
        check_vma=False,
    )
```

```python
import functools

import jax
import jax.numpy as jnp
from jax import lax
from jax.experimental import pallas as pl
from jax.experimental.pallas import tpu as pltpu
from jax.sharding import PartitionSpec as P

OWN = 2


EPS = 1e-05
ROPE_BASE = 500000.0


def rotary_tables(positions, head_dim):
    half_dim = head_dim // 2
    freqs = ROPE_BASE ** (-(jnp.arange(half_dim, dtype=jnp.float32) * 2.0 / head_dim))
    angles = positions[:, None] * freqs[None, :]
    return (jnp.cos(angles), jnp.sin(angles))


def rotate_rows(values, cos_table, sin_table):
    half_dim = values.shape[-1] // 2
    first_half = values[..., :half_dim]
    second_half = values[..., half_dim:]
    return jnp.concatenate(
        [
            first_half * cos_table - second_half * sin_table,
            second_half * cos_table + first_half * sin_table,
        ],
        axis=-1,
    )


def rotate_cols(values, cos_table, sin_table):
    half_dim = values.shape[-2] // 2
    first_half = values[..., :half_dim, :]
    second_half = values[..., half_dim:, :]
    return jnp.concatenate(
        [
            first_half * cos_table - second_half * sin_table,
            second_half * cos_table + first_half * sin_table,
        ],
        axis=-2,
    )


def contract_last(left, right):
    return lax.dot_general(
        left, right, (((1,), (1,)), ((), ())), preferred_element_type=jnp.float32
    )


def contract_first(weights, rows):
    return lax.dot_general(
        weights, rows, (((0,), (1,)), ((), ())), preferred_element_type=jnp.float32
    )


def on_device(
    hidden, gain, w_query, w_key, w_value, cache_pool, prefix_len, hit_page, decode_owner
):
    my_index = lax.axis_index("inst")
    devices = lax.axis_size("inst")
    tok_count = hidden.shape[0]
    head_dim = w_query.shape[1]
    requests = prefix_len.shape[0]
    new_len = tok_count // requests
    gathered = lax.all_gather(hidden, "inst", axis=1, tiled=True)
    wide_vals = gathered.astype(jnp.float32)
    inverse_rms = lax.rsqrt(jnp.mean(wide_vals * wide_vals, axis=-1, keepdims=True) + EPS)
    normed = (wide_vals * inverse_rms * gain).astype(jnp.bfloat16)
    query = jnp.dot(normed, w_query, preferred_element_type=jnp.float32)
    key_cols = contract_first(w_key, normed)
    value_cols = contract_first(w_value, normed)
    new_kv = jnp.stack([key_cols.astype(jnp.bfloat16), value_cols.astype(jnp.bfloat16)])
    all_kv = lax.all_gather(new_kv, "inst", axis=1, tiled=True)
    kv_dim = all_kv.shape[1]
    kv_heads = kv_dim // head_dim
    group_size = devices // kv_heads
    my_group = my_index // group_size
    positions = (
        jnp.repeat(prefix_len, new_len) + jnp.tile(jnp.arange(new_len, dtype=jnp.int32), requests)
    ).astype(jnp.float32)
    cos_table, sin_table = rotary_tables(positions, head_dim)
    q_rot = rotate_rows(query, cos_table, sin_table).astype(jnp.bfloat16)
    k_rot = rotate_cols(
        all_kv[0].astype(jnp.float32).reshape(kv_heads, head_dim, tok_count),
        cos_table.T,
        sin_table.T,
    ).astype(jnp.bfloat16)
    v_heads = all_kv[1].reshape(kv_heads, head_dim, tok_count)
    my_keys = lax.dynamic_index_in_dim(k_rot, my_group, 0, keepdims=False)
    my_values = lax.dynamic_index_in_dim(v_heads, my_group, 0, keepdims=False)
    pool_dev = cache_pool.shape[0]
    page_len = cache_pool.shape[1]
    hit_slots = pool_dev // 2
    flat_hits = hit_page.reshape(-1)
    entries = flat_hits.shape[0]
    is_valid = flat_hits >= 0
    holder = jnp.where(is_valid, flat_hits // pool_dev, -1)
    pool_slot = jnp.where(is_valid, flat_hits % pool_dev, 0)
    entry_ids = jnp.arange(entries, dtype=jnp.int32)
    earlier = (
        (holder[None, :] == holder[:, None])
        & (entry_ids[None, :] < entry_ids[:, None])
        & is_valid[None, :]
    )
    ranking = jnp.sum(earlier.astype(jnp.int32), axis=1)
    mine = is_valid & (holder == my_index)
    chosen = mine[None, :] & (ranking[None, :] == jnp.arange(hit_slots, dtype=jnp.int32)[:, None])
    pool_index = jnp.sum(jnp.where(chosen, pool_slot[None, :], 0), axis=1)
    present = jnp.any(chosen, axis=1)
    picked = cache_pool[pool_index]
    picked = jnp.where(present[:, None, None, None], picked, jnp.zeros_like(picked))
    inv_scale = head_dim ** (-0.5)
    per_head = picked.reshape(hit_slots, page_len, 2, kv_heads, head_dim).transpose(3, 0, 1, 2, 4)
    outgoing = jnp.repeat(per_head, group_size, axis=0)
    incoming = lax.all_to_all(outgoing, "inst", split_axis=0, concat_axis=0, tiled=True)
    stacked = incoming.reshape(devices * hit_slots, page_len, 2, head_dim)
    where_from = jnp.where(is_valid, holder * hit_slots + ranking, 0)
    prefix_rows = stacked[where_from]
    prefix_keys = prefix_rows[:, :, 0].reshape(requests, -1, head_dim)
    prefix_values = prefix_rows[:, :, 1].reshape(requests, -1, head_dim)
    prefix_span = prefix_keys.shape[1]
    causal_ok = (
        jnp.arange(new_len, dtype=jnp.int32)[None, :]
        <= jnp.arange(new_len, dtype=jnp.int32)[:, None]
    )
    pieces = []
    for request in range(requests):
        lower = request * new_len
        q_part = q_rot[lower : lower + new_len]
        pre_scores = contract_last(q_part, prefix_keys[request]) * inv_scale
        new_scores = (
            jnp.dot(q_part, my_keys[:, lower : lower + new_len], preferred_element_type=jnp.float32)
            * inv_scale
        )
        prefix_ok = jnp.arange(prefix_span, dtype=jnp.int32)[None, :] < prefix_len[request]
        row_max = jnp.maximum(
            jnp.max(jnp.where(prefix_ok, pre_scores, -jnp.inf), axis=1),
            jnp.max(jnp.where(causal_ok, new_scores, -jnp.inf), axis=1),
        )[:, None]
        pre_exps = jnp.where(prefix_ok, jnp.exp(pre_scores - row_max), 0.0)
        new_exps = jnp.where(causal_ok, jnp.exp(new_scores - row_max), 0.0)
        row_sum = jnp.sum(pre_exps, axis=1, keepdims=True) + jnp.sum(
            new_exps, axis=1, keepdims=True
        )
        mixture = jnp.dot(
            pre_exps.astype(jnp.bfloat16),
            prefix_values[request],
            preferred_element_type=jnp.float32,
        )
        mixture = mixture + contract_last(
            new_exps.astype(jnp.bfloat16), my_values[:, lower : lower + new_len]
        )
        pieces.append((mixture / row_sum).astype(jnp.bfloat16))
    attn_out = jnp.concatenate(pieces, axis=0)
    pages_new = new_len // page_len
    rows_new = decode_owner.shape[0]
    k_pages = (
        k_rot.reshape(kv_heads, head_dim, requests, pages_new, page_len)
        .transpose(2, 3, 0, 4, 1)
        .reshape(rows_new, page_len, head_dim)
    )
    v_pages = (
        v_heads.reshape(kv_heads, head_dim, requests, pages_new, page_len)
        .transpose(2, 3, 0, 4, 1)
        .reshape(rows_new, page_len, head_dim)
    )
    row_ids = jnp.arange(rows_new, dtype=jnp.int32)
    before_rows = (decode_owner[None, :] == decode_owner[:, None]) & (
        row_ids[None, :] < row_ids[:, None]
    )
    slot_num = jnp.sum(before_rows.astype(jnp.int32), axis=1)
    owned = (decode_owner[None, :] == my_index) & (
        slot_num[None, :] == jnp.arange(OWN, dtype=jnp.int32)[:, None]
    )
    pick_row = jnp.sum(jnp.where(owned, row_ids[None, :], 0), axis=1)
    has_row = jnp.any(owned, axis=1)
    page_pair = jnp.stack([k_pages[pick_row], v_pages[pick_row]], axis=2)
    decode_pages = jnp.where(has_row[:, None, None, None], page_pair, jnp.zeros_like(page_pair))
    return (attn_out, decode_pages)


VMEM_LIMIT = 48 * 1024 * 1024
CHUNK = 1024
SUM_ROWS = 16


def in_vmem(count):
    return [pl.BlockSpec(memory_space=pltpu.VMEM)] * count


def in_smem(count):
    return [pl.BlockSpec(memory_space=pltpu.SMEM)] * count


def params():
    return pltpu.CompilerParams(vmem_limit_bytes=VMEM_LIMIT)


def cost(flops, nbytes):
    return pl.CostEstimate(flops=flops, bytes_accessed=nbytes, transcendentals=0)


def nt_dot(left, right):
    return lax.dot_general(
        left, right, (((1,), (1,)), ((), ())), preferred_element_type=jnp.float32
    )


def holder_of(page, pool_dev):
    if pool_dev & (pool_dev - 1) == 0:
        return jnp.right_shift(page, pool_dev.bit_length() - 1)
    return page // pool_dev


def pick_pages_kernel(place_ref, hits_ref, pool_ref, mine_ref, other_ref, held, sems):
    me, head = place_ref[0], place_ref[1]
    pool_dev, page_len = pool_ref.shape[0], pool_ref.shape[1]
    slots = held.shape[0]
    rows = 2 * page_len
    out_row = lax.broadcasted_iota(jnp.int32, (rows, rows), 0)
    in_row = lax.broadcasted_iota(jnp.int32, (rows, rows), 1)
    wanted = jnp.where(out_row < page_len, 2 * out_row, 2 * (out_row - page_len) + 1)
    unweave = (in_row == wanted).astype(jnp.bfloat16)

    def fetch(page, slot):
        return pltpu.make_async_copy(pool_ref.at[page], held.at[slot], sems.at[slot])

    def entry(e, count):
        page = hits_ref[e]
        is_mine = (page >= 0) & (holder_of(page, pool_dev) == me)

        @pl.when(is_mine)
        def _():
            fetch(page - me * pool_dev, count).start()

        return count + is_mine.astype(jnp.int32)

    count = lax.fori_loop(0, hits_ref.shape[0], entry, jnp.int32(0))

    def arrive(slot, carry):
        fetch(0, slot).wait()
        return carry

    lax.fori_loop(0, count, arrive, 0)
    for slot in range(slots):
        at = slice(slot * rows, (slot + 1) * rows)
        slab = held[slot]
        first = slab[:, :, :128].reshape(rows, 128)
        second = slab[:, :, 128:].reshape(rows, 128)
        both = jnp.concatenate([first, second], axis=1)
        both = jnp.dot(unweave, both, preferred_element_type=jnp.float32)
        both = both.astype(jnp.bfloat16)
        mine_ref[at, :] = jnp.where(head == 0, both[:, :128], both[:, 128:])
        other_ref[at, :] = jnp.where(head == 0, both[:, 128:], both[:, :128])


def pick_pages(place, hits, pool, slots):
    rows = slots * 2 * pool.shape[1]
    block = jax.ShapeDtypeStruct((rows, 128), jnp.bfloat16)
    return pl.pallas_call(
        pick_pages_kernel,
        out_shape=(block, block),
        in_specs=in_smem(2) + [pl.BlockSpec(memory_space=pl.ANY)],
        out_specs=tuple(in_vmem(2)),
        scratch_shapes=[
            pltpu.VMEM((slots,) + pool.shape[1:], jnp.bfloat16),
            pltpu.SemaphoreType.DMA((slots,)),
        ],
        compiler_params=params(),
        cost_estimate=cost(0, 4 * pool.size),
        name="pick_pages",
    )(place, hits, pool)


def column_to_row(column):
    return jnp.transpose(jnp.broadcast_to(column, (128, 128)))[0:1]


def row_to_column(row):
    return jnp.transpose(jnp.broadcast_to(row, (128, 128)))[:, 0:1]


def plane_order(plane):
    return [0, jnp.where(plane <= 2, 1, 3), 2, jnp.where(plane <= 2, 3, 1)]


def pack_weights_kernel(place_ref, wq_ref, wk_ref, wv_ref, own_ref, core_ref, side_ref):
    plane, lane = place_ref[2], place_ref[3]
    feats = wk_ref.shape[0]
    block = wq_ref.shape[0] // 16
    half = own_ref.shape[0]
    for r, out_ref in enumerate((own_ref, core_ref, side_ref, side_ref)):
        base = half if r == 3 else 0
        for k, offset in enumerate(plane_order(plane)):
            start = (((plane + offset) & 3) * 4 + (lane ^ r)) * block
            start = pl.multiple_of(start, block)
            out_ref[base + k * block : base + (k + 1) * block, :] = wq_ref[pl.ds(start, block), :]
            for j in range(block // 128):
                at = base + 4 * block + (k * (block // 128) + j) * 2 * feats
                columns = pl.ds(pl.multiple_of(start + j * 128, 128), 128)
                out_ref[at : at + feats, :] = wk_ref[:, columns]
                out_ref[at + feats : at + 2 * feats, :] = wv_ref[:, columns]


def pack_weights(place, wq, wk_t, wv_t):
    rows = wq.shape[0] // 4 + 2 * wk_t.shape[0] * wk_t.shape[1] // 4 // 128
    block = jax.ShapeDtypeStruct((rows, 128), jnp.bfloat16)
    return pl.pallas_call(
        pack_weights_kernel,
        out_shape=(block, block, jax.ShapeDtypeStruct((2 * rows, 128), jnp.bfloat16)),
        in_specs=in_smem(1) + in_vmem(3),
        out_specs=tuple(in_vmem(3)),
        compiler_params=params(),
        cost_estimate=cost(1, 1),
        name="pack_weights",
    )(place, wq, wk_t, wv_t)


def project_block(k, raw, inv, gain_ref, weights, block):
    chunks = block // 128
    normed = (raw.astype(jnp.float32) * inv * gain_ref[k : k + 1, :]).astype(jnp.bfloat16)
    wide = jnp.concatenate([ref[k * block : (k + 1) * block, :] for ref in weights], axis=1)
    kv_rows = []
    for ref in weights:
        pieces = []
        for j in range(chunks):
            at = 4 * block + (k * chunks + j) * 32
            pieces.append(ref[at : at + 32, :])
        kv_rows.append(jnp.concatenate(pieces, axis=1))
    parts = jnp.dot(normed, wide, preferred_element_type=jnp.float32)
    return parts, nt_dot(jnp.concatenate(kv_rows, axis=0), normed)


def add_sums_kernel(hidden_ref, squares_ref, out_ref):
    toks = hidden_ref.shape[0]
    out_ref[:toks, :] = hidden_ref[...]
    left = squares_ref[...]
    rows = []
    for _ in range(3):
        rows.append(left.astype(jnp.bfloat16).astype(jnp.float32))
        left = left - rows[-1]
    rows.append(jnp.zeros((SUM_ROWS - 3, toks), jnp.float32))
    out_ref[toks:, :] = jnp.concatenate(rows, axis=0).astype(jnp.bfloat16)


def add_sums(hidden, squares):
    toks, block = hidden.shape
    return pl.pallas_call(
        add_sums_kernel,
        out_shape=jax.ShapeDtypeStruct((toks + SUM_ROWS, block), jnp.bfloat16),
        in_specs=in_vmem(2),
        out_specs=in_vmem(1)[0],
        compiler_params=params(),
        cost_estimate=cost(0, 1 << 20),
        name="add_sums",
    )(hidden, squares.reshape(1, toks))


def project_kernel(place_ref, gain_ref, own_ref, *refs):
    downs, ups, weights, out_refs = refs[0:3], refs[3:6], refs[6:10], refs[10:]
    plane = place_ref[2]
    block = own_ref.shape[1]
    toks = own_ref.shape[0] - SUM_ROWS
    sources = (
        lambda at: own_ref[at],
        lambda at: jnp.where(plane <= 2, downs[0][at], ups[0][at]),
        lambda at: jnp.where(plane <= 1, downs[1][at], ups[1][at]),
        lambda at: jnp.where(
            plane == 0, downs[2][at], jnp.where(plane == 3, ups[2][at], ups[0][at])
        ),
    )
    squares = sum(
        jnp.sum(source(slice(toks, toks + SUM_ROWS)).astype(jnp.float32), axis=0, keepdims=True)
        for source in sources
    )
    inv = lax.rsqrt(squares / (block * 16) + EPS)
    inv = jnp.concatenate(
        [row_to_column(inv[:, t : t + 128]) for t in range(0, toks, 128)], axis=0
    )
    query, kv_total = None, None
    for k, source in enumerate(sources):
        parts, kv_part = project_block(k, source(slice(0, toks)), inv, gain_ref, weights, block)
        query = parts if k == 0 else query + parts
        kv_total = kv_part if k == 0 else kv_total + kv_part
    half = toks // 2
    for n, out_ref in enumerate(out_refs):
        r, rows = n // 2, slice(n % 2 * half, (n % 2 + 1) * half)
        out_ref[:half, :] = query[rows, r * 128 : (r + 1) * 128]
        for t in range(half // 128):
            chunk = slice(rows.start + t * 128, rows.start + (t + 1) * 128)
            out_ref[half + t * 32 : half + (t + 1) * 32, :] = kv_total[r * 32 : (r + 1) * 32, chunk]


def project(place, gain, downs, ups, weights):
    toks = downs[0].shape[0] - SUM_ROWS
    out = jax.ShapeDtypeStruct(((toks + 128) // 2, 128), jnp.float32)
    return pl.pallas_call(
        project_kernel,
        out_shape=(out,) * 8,
        in_specs=in_smem(1) + in_vmem(12),
        out_specs=tuple(in_vmem(8)),
        compiler_params=params(),
        cost_estimate=cost(2 * toks * 512 * 640, 6 << 20),
        name="project",
    )(place, gain, *downs, *ups[1:], *weights)


def finish_kernel(*refs):
    cos_ref, sin_ref, out_ref = refs[6:]
    toks = cos_ref.shape[0]
    half, kv_rows = toks // 2, 64
    for n in range(2):
        rows = slice(n * half, (n + 1) * half)
        total = refs[n][...] + refs[2 + n][...] + refs[4 + n][...]
        query = total[:half]
        swapped = jnp.concatenate([query[:, 64:], query[:, :64]], axis=1)
        rotated = query * cos_ref[rows, :] + swapped * sin_ref[rows, :]
        out_ref[rows, :] = rotated.astype(jnp.bfloat16)
        at = toks + n * kv_rows
        out_ref[at : at + kv_rows, :] = total[half:].astype(jnp.bfloat16)


def finish(own, got, far_sum, cos_wide, sin_wide):
    toks = cos_wide.shape[0]
    return pl.pallas_call(
        finish_kernel,
        out_shape=jax.ShapeDtypeStruct((toks + 128, 128), jnp.bfloat16),
        in_specs=in_vmem(8),
        out_specs=in_vmem(1)[0],
        compiler_params=params(),
        cost_estimate=cost(0, 2 << 20),
        name="finish_projection",
    )(*own, *got, *far_sum, cos_wide, sin_wide)


def lane_tiles(values, join):
    joined = values[:, :128]
    for start in range(128, values.shape[1], 128):
        joined = join(joined, values[:, start : start + 128])
    return joined


def put_state(out_ref, toks, first, acc, top, total):
    out_ref[first : first + acc.shape[0], :] = acc
    for b in range(acc.shape[0] // 128):
        row, part = toks + first // 128 + b, slice(b * 128, (b + 1) * 128)
        out_ref[row : row + 1, :] = column_to_row(top[part])
        out_ref[row + 4 : row + 5, :] = column_to_row(total[part])


def get_state(ref, toks, first, count):
    rows = range(toks + first // 128, toks + (first + count) // 128)
    top = [row_to_column(ref[row : row + 1, :]) for row in rows]
    total = [row_to_column(ref[row + 4 : row + 5, :]) for row in rows]
    return ref[first : first + count, :], jnp.concatenate(top), jnp.concatenate(total)


def merge_states(states):
    peak = functools.reduce(jnp.maximum, [top for _, top, _ in states])
    base = jnp.where(peak == -jnp.inf, 0.0, peak)
    fades = [jnp.exp(top - base) for _, top, _ in states]
    acc = sum(acc * fade for (acc, _, _), fade in zip(states, fades))
    total = sum(total * fade for (_, _, total), fade in zip(states, fades))
    return acc, peak, total


def attend_kernel(offset, page_len, earlier, table_ref, *refs):
    blocks, (own_ref, far_ref), refs = refs[:4], refs[4:6], refs[6:]
    before = refs[:2] if earlier else ()
    outs, (held, keys, values, scores_ref, acc, lanes, sems) = refs[-9:-7], refs[-7:]
    copies = [
        pltpu.make_async_copy(block, held.at[n, pl.ds(0, block.shape[0])], sems.at[n])
        for n, block in enumerate(blocks)
    ]
    for copy in copies:
        copy.start()
    me = table_ref[0] ^ offset
    toks = outs[0].shape[0] - 8
    new_len = toks // 2
    chunk_pages = CHUNK // page_len
    for copy in copies:
        copy.wait()
    for request in range(2):
        last_holder = table_ref[1 + request]
        has_last = (last_holder & 12) == (me & 12)
        pages = jnp.int32(0)
        for n in range(4):
            holder = (me & 12) | ((last_holder + 1 + n) & 3)
            count = table_ref[5 + request * 16 + holder]
            first = table_ref[5 + holder] if request else jnp.int32(0)
            which = (holder ^ me) & 3

            def move(p, carry, which=which, first=first, pages=pages):
                source = pl.multiple_of((first + 4 * p) * 2 * page_len, 2 * page_len)
                target = pl.multiple_of((pages + 4 * p) * page_len, page_len)
                slab = held[which, pl.ds(source, 8 * page_len), :]
                slab = slab.reshape(4, 2 * page_len, 128)
                four = pl.ds(target, 4 * page_len)
                keys[four, :] = slab[:, :page_len].reshape(4 * page_len, 128)
                values[four, :] = slab[:, page_len:].reshape(4 * page_len, 128)
                return carry

            lax.fori_loop(0, (count + 3) // 4, move, 0)
            pages = pages + count
        trips = (pages + chunk_pages - 1) // chunk_pages

        rest = pl.ds(pl.multiple_of(pages * page_len, page_len), CHUNK)
        values[rest, :] = jnp.zeros((CHUNK, 128), jnp.bfloat16)
        keys_here = pages * page_len - jnp.where(has_last, table_ref[3 + request], 0)
        rows = slice(request * new_len, (request + 1) * new_len)
        query = jnp.concatenate([far_ref[rows, :], own_ref[rows, :]], axis=0)
        lanes[...] = jnp.full_like(lanes, -jnp.inf)

        def score(n, carry, query=query, keys_here=keys_here):
            at = pl.ds(pl.multiple_of(n * CHUNK, CHUNK), CHUNK)
            scores = nt_dot(query, keys[at, :]) * 128**-0.5
            column = lax.broadcasted_iota(jnp.int32, scores.shape, 1)
            scores = jnp.where(column < keys_here - n * CHUNK, scores, -jnp.inf)
            scores_ref[:, at] = scores
            lanes[...] = jnp.maximum(lanes[...], lane_tiles(scores, jnp.maximum))
            return carry

        lax.fori_loop(0, trips, score, 0)
        top = jnp.max(lanes[...], axis=1, keepdims=True)
        lanes[...] = jnp.zeros_like(lanes)
        acc[...] = jnp.zeros_like(acc)

        def mix(n, carry, top=top):
            at = pl.ds(pl.multiple_of(n * CHUNK, CHUNK), CHUNK)
            exps = jnp.exp(scores_ref[:, at] - top)
            lanes[...] += lane_tiles(exps, jnp.add)
            acc[...] += jnp.dot(
                exps.astype(jnp.bfloat16), values[at, :], preferred_element_type=jnp.float32
            )
            return carry

        lax.fori_loop(0, trips, mix, 0)
        total = jnp.sum(lanes[...], axis=1, keepdims=True)
        for n, out_ref in enumerate(outs):
            part = slice(n * new_len, (n + 1) * new_len)
            state = (acc[part, :], top[part], total[part])
            if earlier:
                past = get_state(before[n], toks, request * new_len, new_len)
                state = merge_states([past, state])
            put_state(out_ref, toks, request * new_len, *state)


def attend(offset, table, blocks, own_query, far_query, earlier, toks, span, page_len):
    new_len = toks // 2
    state = jax.ShapeDtypeStruct((toks + 8, 128), jnp.float32)
    return pl.pallas_call(
        functools.partial(attend_kernel, offset, page_len, bool(earlier)),
        out_shape=(state, state),
        in_specs=in_smem(1)
        + [pl.BlockSpec(memory_space=pl.ANY)] * 4
        + in_vmem(2 + len(earlier)),
        out_specs=tuple(in_vmem(2)),
        scratch_shapes=[
            pltpu.VMEM((4, blocks[0].shape[0] + 8 * page_len, 128), jnp.bfloat16),
            pltpu.VMEM((span + CHUNK, 128), jnp.bfloat16),
            pltpu.VMEM((span + CHUNK, 128), jnp.bfloat16),
            pltpu.VMEM((toks, span), jnp.float32),
            pltpu.VMEM((toks, 128), jnp.float32),
            pltpu.VMEM((toks, 128), jnp.float32),
            pltpu.SemaphoreType.DMA((4,)),
        ],
        compiler_params=params(),
        cost_estimate=cost(1, 20 << 20),
        name="attend_far_plane" if offset else "attend_own_plane",
    )(table, *blocks, own_query, far_query, *earlier)


def new_tokens_kernel(
    place_ref, near_ref, side_ref, core_ref, across_ref, cos_ref, sin_ref, query_ref, state_ref, page_ref, held, kt, vt
):
    me, head = place_ref[0], place_ref[1]
    toks = cos_ref.shape[1]
    for n in range(4):
        held[n] = near_ref[n]
        held[4 + n] = side_ref[n]
        held[8 + n] = core_ref[n]
        held[12 + n] = across_ref[n]
    for device in range(16):
        rel = device ^ me
        block = held[(rel & 1) * 8 + ((rel >> 1) & 1) * 4 + (rel >> 2)]
        rows = slice((device % 8) * 16, (device % 8) * 16 + 16)
        for t in range(toks // 128):
            columns = slice(t * 128, (t + 1) * 128)
            kt[device // 8, rows, columns] = block[t * 32 : t * 32 + 16]
            vt[device // 8, rows, columns] = block[t * 32 + 16 : t * 32 + 32]
    cos, sin = cos_ref[...], sin_ref[...]
    for g in range(2):
        first = kt[g, :64, :].astype(jnp.float32)
        second = kt[g, 64:, :].astype(jnp.float32)
        kt[g, :64, :] = (first * cos - second * sin).astype(jnp.bfloat16)
        kt[g, 64:, :] = (second * cos + first * sin).astype(jnp.bfloat16)
    new_len = toks // 2
    query_at = lax.broadcasted_iota(jnp.int32, (new_len, new_len), 0)
    key_at = lax.broadcasted_iota(jnp.int32, (new_len, new_len), 1)
    for request in range(2):
        part = slice(request * new_len, (request + 1) * new_len)
        scores = jnp.dot(
            query_ref[part, :], kt[head, :, part], preferred_element_type=jnp.float32
        )
        scores = jnp.where(key_at <= query_at, scores * 128**-0.5, -jnp.inf)
        top = jnp.max(scores, axis=1, keepdims=True)
        exps = jnp.exp(scores - top)
        acc = nt_dot(exps.astype(jnp.bfloat16), vt[head, :, part])
        total = jnp.sum(exps, axis=1, keepdims=True)
        put_state(state_ref, toks, request * new_len, acc, top, total)
    page_len = page_ref.shape[1]
    out_row = lax.broadcasted_iota(jnp.int32, (2 * page_len, 128), 0)
    token = lax.broadcasted_iota(jnp.int32, (2 * page_len, 128), 1)
    for slot in range(page_ref.shape[0]):
        row, has = place_ref[4 + 2 * slot], place_ref[5 + 2 * slot]
        start = (row // 8) * (toks // 2) + ((row // 2) % 4) * page_len
        columns = pl.ds(pl.multiple_of(start // 128 * 128, 128), 128)
        inside = token - start % 128
        inside = jnp.where(has > 0, inside, -1)
        take_k = ((out_row % 2 == 0) & (inside == out_row // 2)).astype(jnp.bfloat16)
        take_v = ((out_row % 2 == 1) & (inside == out_row // 2)).astype(jnp.bfloat16)
        woven = nt_dot(take_k, kt[row % 2, :, columns]) + nt_dot(take_v, vt[row % 2, :, columns])
        page_ref[slot] = woven.astype(jnp.bfloat16).reshape(page_len, 2, 128)


def new_tokens(place, near, side, core, across, cos_t, sin_t, query_kv, page_len):
    toks = cos_t.shape[1]
    return pl.pallas_call(
        new_tokens_kernel,
        out_shape=(
            jax.ShapeDtypeStruct((toks + 8, 128), jnp.float32),
            jax.ShapeDtypeStruct((OWN, page_len, 2, 128), jnp.bfloat16),
        ),
        in_specs=in_smem(1) + in_vmem(7),
        out_specs=tuple(in_vmem(2)),
        scratch_shapes=[
            pltpu.VMEM((16, 128, 128), jnp.bfloat16),
            pltpu.VMEM((2, 128, toks), jnp.bfloat16),
            pltpu.VMEM((2, 128, toks), jnp.bfloat16),
        ],
        compiler_params=params(),
        cost_estimate=cost(0, 2 << 20),
        name="new_tokens",
    )(place, near, side, core, across, cos_t, sin_t, query_kv)


def combine_kernel(own_ref, far_ref, new_ref, out_ref):
    toks = out_ref.shape[0]
    for first in range(0, toks, 128):
        states = [get_state(ref, toks, first, 128) for ref in (own_ref, far_ref, new_ref)]
        acc, _, total = merge_states(states)
        out_ref[first : first + 128, :] = (acc / total).astype(jnp.bfloat16)


def combine(own, far, new):
    toks = own.shape[0] - 8
    return pl.pallas_call(
        combine_kernel,
        out_shape=jax.ShapeDtypeStruct((toks, 128), jnp.bfloat16),
        in_specs=in_vmem(3),
        out_specs=in_vmem(1)[0],
        compiler_params=params(),
        cost_estimate=cost(0, 1 << 20),
        name="combine",
    )(own, far, new)


def swap(values, bits):
    return lax.ppermute(values, "inst", [(i, i ^ bits) for i in range(16)])


def after(values, *others):
    return lax.optimization_barrier((values, others))[0]


def hop(values, step, step_count):
    pairs = []
    for i in range(16):
        plane = i // 4
        sends = plane >= step_count - 1 if step > 0 else plane <= 4 - step_count
        if sends and 0 <= plane + step <= 3:
            pairs.append((i, i + 4 * step))
    return lax.ppermute(values, "inst", pairs)


def on_16_devices(
    hidden, gain, w_query, w_key, w_value, cache_pool, prefix_len, hit_page, decode_owner
):
    me = lax.axis_index("inst")
    plane, lane = me // 4, me % 4
    toks, block = hidden.shape
    pool_dev, page_len = cache_pool.shape[0], cache_pool.shape[1]
    requests = prefix_len.shape[0]
    new_len = toks // requests
    slots = pool_dev // 2
    head = me // 8
    rows_new = decode_owner.shape[0]
    row_ids = jnp.arange(rows_new, dtype=jnp.int32)
    before_rows = (decode_owner[None, :] == decode_owner[:, None]) & (
        row_ids[None, :] < row_ids[:, None]
    )
    slot_num = jnp.sum(before_rows.astype(jnp.int32), axis=1)
    owned = (decode_owner[None, :] == me) & (
        slot_num[None, :] == jnp.arange(OWN, dtype=jnp.int32)[:, None]
    )
    pick_row = jnp.sum(jnp.where(owned, row_ids[None, :], 0), axis=1)
    has_row = jnp.any(owned, axis=1).astype(jnp.int32)
    place = jnp.stack([me, head, plane, lane]).astype(jnp.int32)
    page_place = jnp.concatenate([place, jnp.stack([pick_row, has_row], 1).reshape(-1)])
    hits = hit_page.reshape(-1)

    holders = jnp.where(hit_page >= 0, hit_page // pool_dev, -1)
    counts = jnp.sum(
        (holders[:, :, None] == jnp.arange(16, dtype=jnp.int32)).astype(jnp.int32), axis=1
    )
    last_page = (prefix_len - 1) // page_len
    is_last = jnp.arange(hit_page.shape[1], dtype=jnp.int32)[None, :] == last_page[:, None]
    last_holder = jnp.sum(jnp.where(is_last, holders, 0), axis=1)
    missing = (last_page + 1) * page_len - prefix_len
    table = jnp.concatenate([me[None], last_holder, missing, counts.reshape(-1)]).astype(jnp.int32)

    wide = hidden.astype(jnp.float32)
    squares = jnp.sum(wide * wide, axis=1)
    for bit in (1, 2):
        squares = squares + swap(squares, bit)

    w_own, w_core, w_side = pack_weights(place, w_query, w_key.T, w_value.T)
    w_side = swap(after(w_side, squares), 2)
    rows = w_own.shape[0]
    weights = [w_own, swap(w_core, 1), w_side, swap(w_side[rows:], 1)]

    mine, other = pick_pages(place, hits, cache_pool, slots)
    first = add_sums(hidden, squares)
    downs, ups = [first], [first]
    for k in (1, 2, 3):
        down, up = downs[-1], ups[-1]
        if k == 2:
            down, up = after((down, up), mine)
        downs.append(hop(down, -1, k))
        ups.append(hop(up, 1, k))

    mine_side = swap(after(mine, w_side), 2)
    far_pages = swap(after(other, downs[2], ups[2]), 8)

    positions = (
        jnp.repeat(prefix_len, new_len) + jnp.tile(jnp.arange(new_len, dtype=jnp.int32), requests)
    ).astype(jnp.float32)
    cos_table, sin_table = rotary_tables(positions, 128)
    cos_wide = jnp.concatenate([cos_table, cos_table], axis=1)
    sin_wide = jnp.concatenate([-sin_table, sin_table], axis=1)

    gain_blocks = lax.dynamic_index_in_dim(gain.reshape(4, 4, block), lane, 1, keepdims=False)
    gain_blocks = gain_blocks[(plane + jnp.stack(plane_order(plane))) & 3]
    sums = project(place, gain_blocks, downs, ups, weights)
    got = [swap(part, 1) for part in sums[2:4] + sums[6:8]]
    got = after(got, mine_side)
    far_sum = [swap(sums[4 + n] + got[2 + n], 2) for n in range(2)]
    query_kv = finish(sums[:2], got[:2], far_sum, cos_wide, sin_wide)

    far_pages = after(far_pages, far_sum)
    far_side = swap(far_pages, 2)
    near_pages = [mine, swap(mine, 1), mine_side, swap(mine_side, 1)]

    from_plane = swap(query_kv, 4)
    kv = query_kv[toks:]
    pair_kv = jnp.stack([kv, from_plane[toks:]])
    far_kv = swap(pair_kv, 8)

    span = hit_page.shape[1] * page_len
    sizes = (toks, span, page_len)
    part = attend(0, table, near_pages, query_kv, from_plane, (), *sizes)
    near_kv = jnp.concatenate([pair_kv, far_kv], axis=0)
    side_kv = swap(near_kv, 2)
    core_kv, across_kv = swap(near_kv, 1), swap(near_kv, 3)
    away_pages = [far_pages, swap(far_pages, 1), far_side, swap(after(far_side, part), 1)]
    partner_part, own_part = attend(8, table, away_pages, query_kv, from_plane, part, *sizes)
    partner_part = swap(partner_part, 4)
    new_part, decode_pages = new_tokens(
        page_place, near_kv, side_kv, core_kv, across_kv, cos_table.T, sin_table.T, query_kv, page_len
    )
    attn_out = combine(own_part, partner_part, new_part)
    return (attn_out, decode_pages)


def solution(mesh):
    return jax.shard_map(
        on_16_devices if mesh.shape["inst"] == 16 else on_device,
        mesh=mesh,
        in_specs=(
            P("groups", "inst"),
            P(),
            P(None, "inst"),
            P(None, "inst"),
            P(None, "inst"),
            P(("groups", "inst"), None, None, None),
            P("groups"),
            P("groups", None),
            P("groups"),
        ),
        out_specs=(P("groups", "inst"), P(("groups", "inst"), None, None, None)),
        check_vma=False,
    )
```
